512 devices in a mesh: img: 64 (over y, z_lo, x), tpl: 4 (over z_hi), pix: 2 (over core).
Axes of the slice: x: 4, y: 4, z: 16 (z_hi: 4, z_lo: 4; z = z_hi * 4 + z_lo), core: 2. Of those that a mesh axis runs over, the one named last changes fastest.
Arguments:
- images: bfloat16 [16384, 128, 128], P(('img', 'tpl'), 'pix'), may hold values from -6 to 6
- conformers: float32 [8, 3, 4096], replicated, may hold values from -96 to 96
- atom_types: int32 [4096], replicated, may hold values from 0 to 4
- type_amp: float32 [5], replicated, may hold values from 0.3 to 3
- type_width: float32 [5], replicated, may hold values from 0.8 to 2.5
- view_angles: float32 [256, 3], replicated, may hold values from -3.140625 to 3.140625
- template_conf: int32 [512], P(('tpl', 'img')), may hold values from 0 to 7
- template_view: int32 [512], P(('tpl', 'img')), may hold values from 0 to 255
- group_ids: int32 [16384], P('img'), may hold values from 0 to 255
- group_prec: float32 [256], replicated, may hold values from 0.3 to 45
Outputs:
- averages: float32 [512, 128, 128], P(('tpl', 'img'), 'pix')
- loglik: float32 [16384], P(('img', 'tpl'))
The draws below stay inside these ranges and needn't reach their ends.
All inputs are finite; a program needn't handle non-finite values.
Results may differ from the reference program's by a relative error of at most 0.013.
Values may be sent and summed in bfloat16 or wider, within the bound.
A program may use at most 64 MiB of HBM per device.

```python
import math
import jax
import jax.numpy as jnp
from jax import lax

P_SIZE = 128
A = 4096
NTYPE = 5
CONF = 8
VIEWS = 256
GROUPS = 256
TPL = 512
IMAGES = 16384


def draw_group_prec(key, part):
    first_key = jax.random.fold_in(jax.random.fold_in(key, 11), 0)
    values = jnp.exp(jax.random.uniform(first_key, (GROUPS,), jnp.float32, math.log(0.3), math.log(3.0)))
    return values.astype(jnp.float32)


def place_ends(array, key, least, top_value):
    spot = [jax.random.randint(jax.random.fold_in(key, axis), (), 0, length) for axis, length in enumerate(array.shape)]
    widest = array.shape.index(max(array.shape))
    next_to = spot[:widest] + [(spot[widest] + 1) % array.shape[widest]] + spot[widest + 1:]
    return array.at[tuple(spot)].set(least).at[tuple(next_to)].set(top_value)


def block_levels(stream_key, extent, pieces, low, largest):
    factor_of = 1.0
    for position, blocks in pieces:
        draws = jax.random.uniform(jax.random.fold_in(jax.random.fold_in(stream_key, 6), position), (blocks,), jnp.float32, low / len(pieces), largest / len(pieces))
        factor_of = factor_of * jnp.repeat(jnp.exp(draws), extent[position] // blocks).reshape((-1,) + (1,) * (len(extent) - 1 - position))
    return factor_of


def gaussian(key, dims, spread, bound, pieces=(), kind=jnp.bfloat16):
    values = jax.random.normal(key, dims, jnp.float32) * spread
    if len(pieces) > 0:
        values = block_levels(key, dims, pieces, -0.22, 0.18) * values
    return jnp.clip(values, min=-bound, max=bound).astype(kind)


def setup_inputs(seed: int = 0) -> dict:
    key_list = jax.random.split(jax.random.key(seed), 11)
    return {
        "images": gaussian(key_list[0], (IMAGES, P_SIZE, P_SIZE), 1.0, 6.0, ((0, 256), (1, 2))),
        "conformers": gaussian(key_list[1], (CONF, 3, A), (P_SIZE / 8), 96.0, (), jnp.float32),
        "atom_types": place_ends(jax.random.randint(key_list[2], (A,), 0, NTYPE), jax.random.fold_in(key_list[2], 1), 0, NTYPE - 1).astype(jnp.int32),
        "type_amp": jnp.clip(jnp.exp(jax.random.uniform(key_list[3], (NTYPE,), jnp.float32, math.log(0.3), math.log(3.0))), 0.3, 3.0),
        "type_width": jnp.clip(jnp.exp(jax.random.uniform(key_list[4], (NTYPE,), jnp.float32, math.log(0.8), math.log(2.5))), 0.8, 2.5),
        "view_angles": jnp.clip(jax.random.uniform(key_list[5], (VIEWS, 3), jnp.float32, -3.140625, 3.140625), -3.140625, 3.140625),
        "template_conf": place_ends(jax.random.randint(key_list[6], (TPL,), 0, CONF), jax.random.fold_in(key_list[6], 1), 0, CONF - 1).astype(jnp.int32),
        "template_view": place_ends(jax.random.randint(key_list[7], (TPL,), 0, VIEWS), jax.random.fold_in(key_list[7], 1), 0, VIEWS - 1).astype(jnp.int32),
        "group_ids": place_ends(jax.random.randint(key_list[8], (IMAGES,), 0, GROUPS), jax.random.fold_in(key_list[8], 1), 0, GROUPS - 1).astype(jnp.int32),
        "group_prec": draw_group_prec(jax.random.fold_in(key_list[10], 71), 0),
    }


def atom_tables(atom_types, type_amp, type_width):
    hits = atom_types[:, None] == jnp.arange(type_amp.shape[0], dtype=jnp.int32)[None, :]
    atom_amp = lax.optimization_barrier(jnp.sum(jnp.where(hits, type_amp[None, :], 0.0), axis=1)) * 0.0625
    widths = lax.optimization_barrier(jnp.sum(jnp.where(hits, type_width[None, :], 0.0), axis=1))
    return (atom_amp, 0.5 / (widths * widths))

def view_rows(angles):
    cos_phi = jnp.cos(angles[0])
    sin_phi = jnp.sin(angles[0])
    cos_theta = jnp.cos(angles[1])
    sin_theta = jnp.sin(angles[1])
    cos_psi = jnp.cos(angles[2])
    sin_psi = jnp.sin(angles[2])
    first_row = (cos_phi * cos_theta * cos_psi - sin_phi * sin_psi, -cos_phi * cos_theta * sin_psi - sin_phi * cos_psi, cos_phi * sin_theta)
    second_row = (sin_phi * cos_theta * cos_psi + cos_phi * sin_psi, -sin_phi * cos_theta * sin_psi + cos_phi * cos_psi, sin_phi * sin_theta)
    return (first_row, second_row)

def render_one(coords, angles, atom_amp, inv_spread, row_pos, col_pos):
    first_row, second_row = view_rows(angles)
    across = first_row[0] * coords[0] + first_row[1] * coords[1] + first_row[2] * coords[2]
    down = second_row[0] * coords[0] + second_row[1] * coords[1] + second_row[2] * coords[2]
    col_table = jnp.exp(-jnp.square(col_pos[None, :] - across[:, None]) * inv_spread[:, None])
    row_table = atom_amp[:, None] * jnp.exp(-jnp.square(row_pos[None, :] - down[:, None]) * inv_spread[:, None])
    return lax.dot_general(row_table, col_table, (((0,), (0,)), ((), ())), precision=lax.Precision.HIGHEST, preferred_element_type=jnp.float32)

def group_lookup(group_ids, group_prec):
    hits = group_ids[:, None] == jnp.arange(group_prec.shape[0], dtype=jnp.int32)[None, :]
    return lax.optimization_barrier(jnp.sum(jnp.where(hits, group_prec[None, :], 0.0), axis=1))

def reference(images, conformers, atom_types, type_amp, type_width, view_angles, template_conf, template_view, group_ids, group_prec):
    atom_amp, inv_spread = atom_tables(atom_types, type_amp, type_width)
    centres = jnp.arange(P_SIZE).astype(jnp.float32) - P_SIZE * 0.5 + 0.5

    def render_index(index):
        coords = jnp.take(conformers, template_conf[index], axis=0)
        angles = jnp.take(view_angles, template_view[index], axis=0)
        return render_one(coords, angles, atom_amp, inv_spread, centres, centres)
    rendered = lax.map(render_index, jnp.arange(TPL, dtype=jnp.int32))
    rendered = rendered.astype(jnp.bfloat16).reshape(TPL, P_SIZE * P_SIZE)
    norms = lax.optimization_barrier(jnp.sum(jnp.square(rendered.astype(jnp.float32)), axis=1))
    flat_images = images.reshape(IMAGES, P_SIZE * P_SIZE)
    scores = lax.dot_general(flat_images, rendered, (((1,), (1,)), ((), ())), preferred_element_type=jnp.float32)
    precision_rows = group_lookup(group_ids, group_prec)
    logits = precision_rows[:, None] * scores * lax.rsqrt(norms + 1e-06)[None, :]
    maximum = lax.optimization_barrier(jnp.max(logits, axis=1))
    weights = jnp.exp(logits - maximum[:, None])
    totals = lax.optimization_barrier(jnp.sum(weights, axis=1))
    loglik = maximum + jnp.log(totals)
    resp = (weights / totals[:, None]).astype(jnp.bfloat16)
    sums = lax.dot_general(resp, flat_images, (((0,), (0,)), ((), ())), preferred_element_type=jnp.float32)
    scale = lax.rsqrt(lax.optimization_barrier(jnp.mean(jnp.square(sums), axis=1)) + 1e-06)
    return ((sums * scale[:, None]).reshape(TPL, P_SIZE, P_SIZE), loglik)
```

```python
import functools

import jax
import jax.numpy as jnp
from jax import lax
from jax.experimental import pallas as pl
from jax.experimental.pallas import tpu as pltpu
from jax.sharding import PartitionSpec as P

NX, NY, NZL = 4, 4, 4
MESH = pl.DeviceIdType.MESH
NT = (((1,), (1,)), ((), ()))


def view_rows(angles):
    cos_phi = jnp.cos(angles[0])
    sin_phi = jnp.sin(angles[0])
    cos_theta = jnp.cos(angles[1])
    sin_theta = jnp.sin(angles[1])
    cos_psi = jnp.cos(angles[2])
    sin_psi = jnp.sin(angles[2])
    return (
        cos_phi * cos_theta * cos_psi - sin_phi * sin_psi,
        -cos_phi * cos_theta * sin_psi - sin_phi * cos_psi,
        cos_phi * sin_theta,
        sin_phi * cos_theta * cos_psi + cos_phi * sin_psi,
        -sin_phi * cos_theta * sin_psi + cos_phi * cos_psi,
        sin_phi * sin_theta,
    )


def group_lookup(group_ids, group_prec):
    hits = group_ids[:, None] == jnp.arange(group_prec.shape[0], dtype=jnp.int32)[None, :]
    return jnp.sum(jnp.where(hits, group_prec[None, :], 0.0), axis=1)


def em_kernel(
    side,
    kc,
    rows_sm,
    conf_sm,
    tamp_sm,
    twid_sm,
    images,
    conformers,
    types,
    prec,
    out,
    loglik,
    img_buf,
    tsend,
    tbuf,
    tall,
    ssend,
    srecv,
    lsend,
    lrecv,
    rall,
    sums,
    rsf_send,
    rsf_recv,
    rsb_send,
    rsb_recv,
    fsend,
    fin,
    stage,
    orecv,
    acc,
    i_s,
    i_r,
    x_s,
    x_r,
    t_s,
    t_r,
    af_s,
    af_r,
    ab_s,
    ab_r,
    s_s,
    s_r,
    l_s,
    l_r,
    r_s,
    r_r,
    rf_s,
    rf_r,
    rb_s,
    rb_r,
    f_s,
    f_r,
    o_s,
    o_r,
    own_sem,
):
    plane = NX * NY
    img = lax.axis_index("img")
    tpl = lax.axis_index("tpl")
    pix = lax.axis_index("pix")
    nz = NZL * lax.axis_size("tpl")
    x = lax.rem(img, NX)
    zl = lax.rem(lax.div(img, NX), NZL)
    y = lax.div(img, NX * NZL)
    z = tpl * NZL + zl
    me = y * NX + x
    half_rows = side // 2
    part_rows = half_rows // plane
    part = part_rows * side
    tile_rows = 2 * part_rows
    nimg = images.shape[0]
    fwd = nz // 2
    bwd = nz - 1 - fwd

    def mate(q):
        qy = lax.div(q, NX)
        qx = lax.rem(q, NX)
        return ((qy * NZL + zl) * NX + qx, tpl, pix)

    def along(step):
        zz = lax.rem(z + step + nz, nz)
        zt = lax.div(zz, NZL)
        zr = lax.rem(zz, NZL)
        return ((y * NZL + zr) * NX + x, zt, pix)

    up, down = along(1), along(-1)
    twin = (img, tpl, 1 - pix)

    def other(d):
        return lax.rem(me + d, plane)

    def rows_of(q):
        return pl.ds(pl.multiple_of(q * tile_rows, tile_rows), tile_rows)

    def remote(src, dst, ss, rs, dev):
        return pltpu.make_async_remote_copy(
            src_ref=src, dst_ref=dst, send_sem=ss, recv_sem=rs, device_id=dev, device_id_type=MESH
        )

    def each(body):
        @pl.loop(1, plane)
        def _(d):
            body(other(d))

    bar = pltpu.get_barrier_semaphore()
    each(lambda q: pl.semaphore_signal(bar, inc=1, device_id=mate(q), device_id_type=MESH))
    for dev in (up, down, twin):
        pl.semaphore_signal(bar, inc=1, device_id=dev, device_id_type=MESH)
    pl.semaphore_wait(bar, plane - 1 + 3)

    def image_copy(q, src_of):
        cols = pl.ds(pl.multiple_of(q * part, part), part)
        return remote(
            images.at[:, cols], img_buf.at[pix, src_of], i_s.at[q], i_r.at[src_of], mate(q)
        )

    each(lambda q: image_copy(q, me).start())
    own = pltpu.make_async_copy(
        images.at[:, pl.ds(pl.multiple_of(me * part, part), part)], img_buf.at[pix, me], own_sem
    )
    own.start()

    conf = conf_sm[pix]
    s_idx = lax.broadcasted_iota(jnp.int32, (side, 1), 0)
    owner = s_idx // tile_rows
    in_tile = lax.rem(s_idx, tile_rows)
    row_id = (in_tile // part_rows) * half_rows + owner * part_rows + lax.rem(in_tile, part_rows)
    row_pos = row_id.astype(jnp.float32) - side * 0.5 + 0.5
    col_pos = s_idx.astype(jnp.float32) - side * 0.5 + 0.5
    acc[...] = jnp.zeros_like(acc)

    @pl.loop(0, types.shape[1] // kc)
    def _(k):
        sl = pl.ds(pl.multiple_of(k * kc, kc), kc)
        kind = types[:, sl]
        amp = jnp.zeros((1, kc), jnp.float32)
        width = jnp.zeros((1, kc), jnp.float32)
        for j in range(tamp_sm.shape[0]):
            amp = jnp.where(kind == j, tamp_sm[j], amp)
            width = jnp.where(kind == j, twid_sm[j], width)
        amp = amp * 0.0625
        spread = 0.5 / (width * width)
        c0 = conformers[conf, 0:1, sl]
        c1 = conformers[conf, 1:2, sl]
        c2 = conformers[conf, 2:3, sl]
        across = rows_sm[0] * c0 + rows_sm[1] * c1 + rows_sm[2] * c2
        below = rows_sm[3] * c0 + rows_sm[4] * c1 + rows_sm[5] * c2
        dc = col_pos - across
        dr = row_pos - below
        col = jnp.exp(-(dc * dc) * spread)
        row = amp * jnp.exp(-(dr * dr) * spread)
        col_hi = col.astype(jnp.bfloat16)
        col_lo = (col - col_hi.astype(jnp.float32)).astype(jnp.bfloat16)
        row_hi = row.astype(jnp.bfloat16)
        row_lo = (row - row_hi.astype(jnp.float32)).astype(jnp.bfloat16)
        total = lax.dot_general(row_hi, col_lo, NT, preferred_element_type=jnp.float32)
        total += lax.dot_general(row_lo, col_hi, NT, preferred_element_type=jnp.float32)
        total += lax.dot_general(row_hi, col_hi, NT, preferred_element_type=jnp.float32)
        acc[...] += total

    tsend[...] = acc[...].astype(jnp.bfloat16).astype(jnp.float32)

    def template_copy(q, src_of):
        return remote(tsend.at[rows_of(q)], tbuf.at[rows_of(src_of)], t_s.at[q], t_r.at[src_of], mate(q))

    each(lambda q: template_copy(q, me).start())
    tbuf[rows_of(me), :] = tsend[rows_of(me), :]
    each(lambda q: template_copy(q, q).wait_recv())
    for k in range(tile_rows):
        tall[z, :, k * side : (k + 1) * side] = tbuf[pl.ds(k, plane, stride=tile_rows), :].astype(
            jnp.bfloat16
        )

    def up_block(s, first):
        b = lax.rem(first - s + 2 * nz, nz)
        return remote(tall.at[b], tall.at[b], af_s.at[s], af_r.at[s], up)

    def down_block(s, first):
        b = lax.rem(first + s, nz)
        return remote(tall.at[b], tall.at[b], ab_s.at[s], ab_r.at[s], down)

    swap = remote(img_buf.at[pix], img_buf.at[pix], x_s, x_r, twin)
    for s in range(fwd):
        if s > 0:
            up_block(s - 1, z - 1).wait_recv()
        up_block(s, z).start()
        if s < bwd:
            if s > 0:
                down_block(s - 1, z + 1).wait_recv()
            down_block(s, z).start()
        if s == min(2, fwd - 1):
            own.wait()
            each(lambda q: image_copy(q, q).wait_recv())
            swap.start()
    up_block(fwd - 1, z - 1).wait_recv()
    if bwd > 0:
        down_block(bwd - 1, z + 1).wait_recv()
    remote(img_buf.at[1 - pix], img_buf.at[1 - pix], x_s, x_r, twin).wait_recv()

    ntpl = nz * plane
    both = tall[...].reshape(ntpl, 2 * part)
    tf = both.astype(jnp.float32)
    sq = tf * tf
    sq_hi = sq.astype(jnp.bfloat16)
    sq_lo = (sq - sq_hi.astype(jnp.float32)).astype(jnp.bfloat16)
    ones = jnp.ones((8, 2 * part), jnp.bfloat16)
    norm = lax.dot_general(ones, sq_hi, NT, preferred_element_type=jnp.float32)
    norm += lax.dot_general(ones, sq_lo, NT, preferred_element_type=jnp.float32)

    def score_copy(q, src_of):
        return remote(ssend.at[q], srecv.at[src_of], s_s.at[q], s_r.at[src_of], mate(q))

    group = 4

    @pl.loop(0, plane // group)
    def _(g):
        at = pl.ds(g * group, group)
        lhs = img_buf[0, at].reshape(group * nimg, part)
        res = lax.dot_general(lhs, tall[:, :, :part].reshape(ntpl, part), NT, preferred_element_type=jnp.float32)
        lhs = img_buf[1, at].reshape(group * nimg, part)
        res += lax.dot_general(lhs, tall[:, :, part:].reshape(ntpl, part), NT, preferred_element_type=jnp.float32)
        ssend[at, :nimg, :] = res.reshape(group, nimg, ntpl)
        ssend[at, nimg:, :] = jnp.broadcast_to(norm[None], (group, 8, ntpl))

    each(lambda q: score_copy(q, me).start())
    each(lambda q: score_copy(q, q).wait_recv())
    srecv[pl.ds(me, 1)] = ssend[pl.ds(me, 1)]
    full = jnp.sum(srecv[...], axis=0)
    logits = prec[...] * full[:nimg] * lax.rsqrt(full[nimg : nimg + 1] + 1e-06)
    lsend[...] = logits
    logit_copy = remote(lsend, lrecv, l_s, l_r, twin)
    logit_copy.start()
    logit_copy.wait_recv()
    theirs = lrecv[...]
    top = jnp.maximum(
        jnp.max(logits, axis=1, keepdims=True), jnp.max(theirs, axis=1, keepdims=True)
    )
    weights = jnp.exp(logits - top)
    totals = jnp.sum(weights, axis=1, keepdims=True) + jnp.sum(
        jnp.exp(theirs - top), axis=1, keepdims=True
    )
    loglik[...] = top + jnp.log(totals)
    rall[pl.ds(me, 1)] = (weights / totals).astype(jnp.bfloat16)[None]

    def resp_copy(q, src_of):
        return remote(rall.at[src_of], rall.at[src_of], r_s.at[q], r_r.at[src_of], mate(q))

    each(lambda q: resp_copy(q, me).start())
    each(lambda q: resp_copy(q, q).wait_recv())

    resp = rall[...].reshape(plane * nimg, ntpl).astype(jnp.float32).T.astype(jnp.bfloat16)
    for h in range(2):
        res = lax.dot_general(
            resp,
            img_buf[h].reshape(plane * nimg, part),
            (((1,), (0,)), ((), ())),
            preferred_element_type=jnp.float32,
        )
        sums[:, :, h * part : (h + 1) * part] = res.reshape(nz, plane, part)

    for s in range(fwd):
        val = sums[lax.rem(z + fwd - s, nz)]
        if s > 0:
            remote(rsf_send.at[s - 1], rsf_recv.at[s - 1], rf_s.at[s - 1], rf_r.at[s - 1], up).wait_recv()
            val = val + rsf_recv[s - 1].astype(jnp.float32)
        rsf_send[s] = val.astype(jnp.bfloat16)
        remote(rsf_send.at[s], rsf_recv.at[s], rf_s.at[s], rf_r.at[s], up).start()
        if s < bwd:
            val = sums[lax.rem(z - bwd + s + nz, nz)]
            if s > 0:
                remote(rsb_send.at[s - 1], rsb_recv.at[s - 1], rb_s.at[s - 1], rb_r.at[s - 1], down).wait_recv()
                val = val + rsb_recv[s - 1].astype(jnp.float32)
            rsb_send[s] = val.astype(jnp.bfloat16)
            remote(rsb_send.at[s], rsb_recv.at[s], rb_s.at[s], rb_r.at[s], down).start()
    val = sums[z]
    remote(rsf_send.at[fwd - 1], rsf_recv.at[fwd - 1], rf_s.at[fwd - 1], rf_r.at[fwd - 1], up).wait_recv()
    val = val + rsf_recv[fwd - 1].astype(jnp.float32)
    if bwd > 0:
        remote(rsb_send.at[bwd - 1], rsb_recv.at[bwd - 1], rb_s.at[bwd - 1], rb_r.at[bwd - 1], down).wait_recv()
        val = val + rsb_recv[bwd - 1].astype(jnp.float32)
    for k in range(tile_rows):
        fsend[pl.ds(k, plane, stride=tile_rows), :] = val[:, k * side : (k + 1) * side]

    def final_copy(q, src_of):
        return remote(fsend.at[rows_of(q)], fin.at[rows_of(src_of)], f_s.at[q], f_r.at[src_of], mate(q))

    each(lambda q: final_copy(q, me).start())
    fin[rows_of(me), :] = fsend[rows_of(me), :]
    each(lambda q: final_copy(q, q).wait_recv())
    whole = fin[...]
    squares = jnp.sum(jnp.sum(whole * whole, axis=1, keepdims=True), axis=0, keepdims=True)
    scaled = whole * lax.rsqrt(squares / (side * side) + 1e-06)
    for q in range(plane):
        for h in range(2):
            at = q * tile_rows + h * part_rows
            stage[h, q * part_rows : (q + 1) * part_rows, :] = scaled[at : at + part_rows, :]
    half_copy = remote(stage.at[1 - pix], orecv, o_s, o_r, twin)
    half_copy.start()
    out[pl.ds(pix, 1)] = stage[pl.ds(pix, 1)]
    half_copy.wait_recv()
    out[pl.ds(1 - pix, 1)] = orecv[...][None]

    each(lambda q: image_copy(q, me).wait_send())
    each(lambda q: template_copy(q, me).wait_send())
    each(lambda q: score_copy(q, me).wait_send())
    each(lambda q: resp_copy(q, me).wait_send())
    each(lambda q: final_copy(q, me).wait_send())
    swap.wait_send()
    logit_copy.wait_send()
    half_copy.wait_send()
    for s in range(fwd):
        up_block(s, z).wait_send()
        remote(rsf_send.at[s], rsf_recv.at[s], rf_s.at[s], rf_r.at[s], up).wait_send()
    for s in range(bwd):
        down_block(s, z).wait_send()
        remote(rsb_send.at[s], rsb_recv.at[s], rb_s.at[s], rb_r.at[s], down).wait_send()


def on_device(
    images,
    conformers,
    atom_types,
    type_amp,
    type_width,
    view_angles,
    template_conf,
    template_view,
    group_ids,
    group_prec,
):
    nimg, half_rows, side = images.shape
    plane = NX * NY
    nz = NZL * lax.axis_size("tpl")
    part = half_rows * side // plane
    ntpl = nz * plane
    fwd = nz // 2
    bwd = max(nz - 1 - fwd, 1)
    flat = images.reshape(nimg, half_rows * side)
    pix = lax.axis_index("pix")
    angles = jnp.take(view_angles, lax.dynamic_index_in_dim(template_view, pix, keepdims=False), axis=0)
    rows = jnp.stack(view_rows(angles))
    own_ids = lax.dynamic_slice_in_dim(group_ids, lax.axis_index("tpl") * nimg, nimg)
    prec = group_lookup(own_ids, group_prec)[:, None]
    bf16, f32 = jnp.bfloat16, jnp.float32
    vmem = pl.BlockSpec(memory_space=pltpu.VMEM)
    smem = pl.BlockSpec(memory_space=pltpu.SMEM)
    dma = pltpu.SemaphoreType.DMA
    natoms = atom_types.shape[0]
    averages, loglik = pl.pallas_call(
        functools.partial(em_kernel, side, min(512, natoms)),
        out_shape=(
            jax.ShapeDtypeStruct((2, half_rows, side), f32),
            jax.ShapeDtypeStruct((nimg, 1), f32),
        ),
        in_specs=[smem] * 4 + [vmem] * 4,
        out_specs=(vmem, vmem),
        scratch_shapes=[
            pltpu.VMEM((2, plane, nimg, part), bf16),
            pltpu.VMEM((side, side), f32),
            pltpu.VMEM((side, side), f32),
            pltpu.VMEM((nz, plane, 2 * part), bf16),
            pltpu.VMEM((plane, nimg + 8, ntpl), f32),
            pltpu.VMEM((plane, nimg + 8, ntpl), f32),
            pltpu.VMEM((nimg, ntpl), f32),
            pltpu.VMEM((nimg, ntpl), f32),
            pltpu.VMEM((plane, nimg, ntpl), bf16),
            pltpu.VMEM((nz, plane, 2 * part), f32),
            pltpu.VMEM((fwd, plane, 2 * part), bf16),
            pltpu.VMEM((fwd, plane, 2 * part), bf16),
            pltpu.VMEM((bwd, plane, 2 * part), bf16),
            pltpu.VMEM((bwd, plane, 2 * part), bf16),
            pltpu.VMEM((side, side), f32),
            pltpu.VMEM((side, side), f32),
            pltpu.VMEM((2, half_rows, side), f32),
            pltpu.VMEM((half_rows, side), f32),
            pltpu.VMEM((side, side), f32),
            dma((plane,)),
            dma((plane,)),
            dma,
            dma,
            dma((plane,)),
            dma((plane,)),
            dma((fwd,)),
            dma((fwd,)),
            dma((bwd,)),
            dma((bwd,)),
            dma((plane,)),
            dma((plane,)),
            dma,
            dma,
            dma((plane,)),
            dma((plane,)),
            dma((fwd,)),
            dma((fwd,)),
            dma((bwd,)),
            dma((bwd,)),
            dma((plane,)),
            dma((plane,)),
            dma,
            dma,
            dma,
        ],
        compiler_params=pltpu.CompilerParams(
            collective_id=0, has_side_effects=True, vmem_limit_bytes=48 * 1024 * 1024
        ),
    )(
        rows,
        template_conf,
        type_amp,
        type_width,
        flat,
        conformers,
        atom_types[None, :],
        prec,
    )
    return averages, loglik[:, 0]


def solution(mesh):
    placed = (
        P(("img", "tpl"), "pix", None),
        P(),
        P(),
        P(),
        P(),
        P(),
        P(("tpl", "img")),
        P(("tpl", "img")),
        P("img"),
        P(),
    )
    return jax.shard_map(
        on_device,
        mesh=mesh,
        in_specs=placed,
        out_specs=(P(("tpl", "img"), "pix", None), P(("img", "tpl"))),
        check_vma=False,
    )
```

```python
import functools

import jax
import jax.numpy as jnp
from jax import lax
from jax.experimental import pallas as pl
from jax.experimental.pallas import tpu as pltpu
from jax.sharding import PartitionSpec as P

NX, NY, NZL = 4, 4, 4
MESH = pl.DeviceIdType.MESH
NT = (((1,), (1,)), ((), ()))


EARLY = (0, 1, 2, 3, 4, 12, 14, 15)
LATE = (8, 7, 9, 5, 6, 10, 11, 13)
ORDER = EARLY + LATE
POS = {k: i for i, k in enumerate(ORDER)}
NZ = 16
RELAY = {0: ((1, -1), (15, 1), (2, -2), (14, 2)), 4: ((5, -1), (3, 1), (6, -2)), 12: ((13, -1), (11, 1), (10, 2)), 8: ((9, -1), (7, 1))}
STEPS = (1, -1, 2, -2, 4, -4, 8)


def em_kernel(
    side,
    kc,
    conf_sm,
    view_sm,
    tamp_sm,
    twid_sm,
    images,
    conformers,
    types,
    angles,
    ids,
    group_prec,
    out,
    loglik,
    img_buf,
    tsend,
    tbuf,
    tall,
    ssend,
    srecv,
    lsend,
    lrecv,
    rall,
    own_sums,
    sums,
    rr,
    r2_send,
    r2_recv,
    fsend,
    fin,
    stage,
    orecv,
    acc,
    i_s,
    i_r,
    x_s,
    x_r,
    t_s,
    t_r,
    a_s,
    a_r,
    s_s,
    s_r,
    l_s,
    l_r,
    r_s,
    r_r,
    z_s,
    z_r,
    z2_s,
    z2_r,
    f_s,
    f_r,
    o_s,
    o_r,
    own_sem,
):
    f32, bf16 = jnp.float32, jnp.bfloat16
    plane = NX * NY
    img = lax.axis_index("img")
    tpl = lax.axis_index("tpl")
    pix = lax.axis_index("pix")
    x = lax.rem(img, NX)
    zl = lax.rem(lax.div(img, NX), NZL)
    y = lax.div(img, NX * NZL)
    z = tpl * NZL + zl
    me = y * NX + x
    half_rows = side // 2
    part_rows = half_rows // plane
    part = part_rows * side
    tile_rows = 2 * part_rows
    nimg = images.shape[1]
    half = len(EARLY)
    ntpl = half * plane

    def mate(q):
        qy = lax.div(q, NX)
        qx = lax.rem(q, NX)
        return ((qy * NZL + zl) * NX + qx, tpl, pix)

    def along(step):
        zz = lax.rem(z + step + NZ, NZ)
        zt = lax.div(zz, NZL)
        zr = lax.rem(zz, NZL)
        return ((y * NZL + zr) * NX + x, zt, pix)

    twin = (img, tpl, 1 - pix)

    def rows_of(q):
        return pl.ds(pl.multiple_of(q * tile_rows, tile_rows), tile_rows)

    def remote(src, dst, ss, rs, dev):
        return pltpu.make_async_remote_copy(
            src_ref=src, dst_ref=dst, send_sem=ss, recv_sem=rs, device_id=dev, device_id_type=MESH
        )

    def each(body, first=1, last=plane):
        @pl.loop(first, last)
        def _(d):
            body(lax.rem(me + d, plane))

    bar = pltpu.get_barrier_semaphore()
    each(lambda q: pl.semaphore_signal(bar, inc=1, device_id=mate(q), device_id_type=MESH))
    for step in STEPS:
        pl.semaphore_signal(bar, inc=1, device_id=along(step), device_id_type=MESH)
    pl.semaphore_signal(bar, inc=1, device_id=twin, device_id_type=MESH)

    own = pltpu.make_async_copy(images.at[me], img_buf.at[pix, me], own_sem)
    own.start()

    conf = conf_sm[pix]
    view = angles[pl.ds(view_sm[pix], 1), :]
    cosines = jnp.cos(view)
    sines = jnp.sin(view)
    cos_phi, cos_theta, cos_psi = (cosines[:, i : i + 1] for i in range(3))
    sin_phi, sin_theta, sin_psi = (sines[:, i : i + 1] for i in range(3))
    r00 = cos_phi * cos_theta * cos_psi - sin_phi * sin_psi
    r01 = -cos_phi * cos_theta * sin_psi - sin_phi * cos_psi
    r02 = cos_phi * sin_theta
    r10 = sin_phi * cos_theta * cos_psi + cos_phi * sin_psi
    r11 = -sin_phi * cos_theta * sin_psi + cos_phi * cos_psi
    r12 = sin_phi * sin_theta
    s_idx = lax.broadcasted_iota(jnp.int32, (side, 1), 0)
    owner = s_idx // tile_rows
    in_tile = lax.rem(s_idx, tile_rows)
    row_id = (in_tile // part_rows) * half_rows + owner * part_rows + lax.rem(in_tile, part_rows)
    row_pos = row_id.astype(f32) - side * 0.5 + 0.5
    col_pos = s_idx.astype(f32) - side * 0.5 + 0.5
    acc[...] = jnp.zeros_like(acc)

    @pl.loop(0, types.shape[1] // kc)
    def _(k):
        sl = pl.ds(pl.multiple_of(k * kc, kc), kc)
        kind = types[:, sl]
        amp = jnp.zeros((1, kc), f32)
        width = jnp.zeros((1, kc), f32)
        for j in range(tamp_sm.shape[0]):
            amp = jnp.where(kind == j, tamp_sm[j], amp)
            width = jnp.where(kind == j, twid_sm[j], width)
        amp = amp * 0.0625
        spread = 0.5 / (width * width)
        c0 = conformers[conf, 0:1, sl]
        c1 = conformers[conf, 1:2, sl]
        c2 = conformers[conf, 2:3, sl]
        across = r00 * c0 + r01 * c1 + r02 * c2
        below = r10 * c0 + r11 * c1 + r12 * c2
        dc = col_pos - across
        dr = row_pos - below
        col = jnp.exp(-(dc * dc) * spread)
        row = amp * jnp.exp(-(dr * dr) * spread)
        col_hi = col.astype(bf16)
        col_lo = (col - col_hi.astype(f32)).astype(bf16)
        row_hi = row.astype(bf16)
        row_lo = (row - row_hi.astype(f32)).astype(bf16)
        total = lax.dot_general(row_hi, col_lo, NT, preferred_element_type=f32)
        total += lax.dot_general(row_lo, col_hi, NT, preferred_element_type=f32)
        total += lax.dot_general(row_hi, col_hi, NT, preferred_element_type=f32)
        acc[...] += total

    tsend[...] = acc[...].astype(bf16).astype(f32)

    groups = ids.shape[1]
    at_row = lax.broadcasted_iota(jnp.int32, (nimg, groups), 0)
    at_col = lax.broadcasted_iota(jnp.int32, (nimg, groups), 1)
    own_id = jnp.sum(
        jnp.where(at_col == at_row + tpl * nimg, ids[...].astype(f32), 0.0), axis=1, keepdims=True
    )
    ngrp = group_prec.shape[1]
    grp = lax.broadcasted_iota(jnp.int32, (nimg, ngrp), 1).astype(f32)
    prec = jnp.sum(jnp.where(grp == own_id, group_prec[...], 0.0), axis=1, keepdims=True)

    pl.semaphore_wait(bar, plane - 1 + len(STEPS) + 1)

    def template_copy(q, src_of):
        return remote(tsend.at[rows_of(q)], tbuf.at[rows_of(src_of)], t_s.at[q], t_r.at[src_of], mate(q))

    each(lambda q: template_copy(q, me).start())

    def image_copy(q, src_of):
        return remote(images.at[q], img_buf.at[pix, src_of], i_s.at[q], i_r.at[src_of], mate(q))

    each(lambda q: image_copy(q, me).start())

    def swap(q, h):
        return remote(img_buf.at[h, q], img_buf.at[h, q], x_s.at[q], x_r.at[q], twin)

    own.wait()
    swap(me, pix).start()

    tbuf[rows_of(me), :] = tsend[rows_of(me), :]
    each(lambda q: template_copy(q, q).wait_recv())
    for k in range(tile_rows):
        tall[POS[0], :, k * side : (k + 1) * side] = tbuf[
            pl.ds(k, plane, stride=tile_rows), :
        ].astype(bf16)

    def block(src, dst, step):
        return remote(tall.at[POS[src]], tall.at[POS[dst]], a_s.at[dst], a_r.at[dst], along(step))

    def arrived(dst):
        block(dst, dst, 0).wait_recv()

    moves = [(0, 8, 8), (0, 12, 4), (0, 4, -4)]
    for src in (0, 4, 12, 8):
        moves += [(src, dst, step) for dst, step in RELAY[src]]

    def start_from(src):
        for m in moves:
            if m[0] == src:
                block(*m).start()

    start_from(0)
    middle = plane // 2 + 1

    def pass_image(q):
        image_copy(q, q).wait_recv()
        swap(q, pix).start()

    arrived(4)
    start_from(4)
    arrived(12)
    start_from(12)
    each(pass_image, 1, middle)
    arrived(8)
    start_from(8)
    each(pass_image, middle, plane)
    for k in EARLY:
        if k not in (0, 4, 12):
            arrived(k)
    each(lambda q: swap(q, 1 - pix).wait_recv(), 0, plane)

    def score_copy(h, q, src_of):
        return remote(ssend.at[h, q], srecv.at[h, src_of], s_s.at[h, q], s_r.at[h, src_of], mate(q))

    group = 4

    def score_half(h):
        planes = tall[h * half : (h + 1) * half].reshape(ntpl, 2 * part)
        tf = planes.astype(f32)
        sq = tf * tf
        sq_hi = sq.astype(bf16)
        sq_lo = (sq - sq_hi.astype(f32)).astype(bf16)
        ones = jnp.ones((8, 2 * part), bf16)
        norm = lax.dot_general(ones, sq_hi, NT, preferred_element_type=f32)
        norm += lax.dot_general(ones, sq_lo, NT, preferred_element_type=f32)

        @pl.loop(0, plane // group)
        def _(g):
            at = pl.ds(g * group, group)
            res = jnp.broadcast_to(jnp.zeros((1, 1), f32), (group * nimg, ntpl))
            for c in range(2):
                res += lax.dot_general(
                    img_buf[c, at].reshape(group * nimg, part),
                    tall[h * half : (h + 1) * half, :, c * part : (c + 1) * part].reshape(ntpl, part),
                    NT,
                    preferred_element_type=f32,
                )
            ssend[h, at, :nimg, :] = res.reshape(group, nimg, ntpl)
            ssend[h, at, nimg:, :] = jnp.broadcast_to(norm[None], (group, 8, ntpl))

        each(lambda q: score_copy(h, q, me).start())
        srecv[h, pl.ds(me, 1)] = ssend[h, pl.ds(me, 1)]

    score_half(0)
    for k in LATE:
        if k != 8:
            arrived(k)
    score_half(1)

    def logit_copy(h):
        return remote(lsend.at[h], lrecv.at[h], l_s.at[h], l_r.at[h], twin)

    for h in range(2):
        each(lambda q: score_copy(h, q, q).wait_recv())
        full = jnp.sum(srecv[h], axis=0)
        lsend[h] = prec * full[:nimg] * lax.rsqrt(full[nimg : nimg + 1] + 1e-06)
        logit_copy(h).start()
    own_top = jnp.max(jnp.maximum(lsend[0], lsend[1]), axis=1, keepdims=True)
    for h in range(2):
        logit_copy(h).wait_recv()
    top = jnp.maximum(
        own_top, jnp.max(jnp.maximum(lrecv[0], lrecv[1]), axis=1, keepdims=True)
    )
    weights = [jnp.exp(lsend[h] - top) for h in range(2)]
    totals = jnp.sum(weights[0] + weights[1], axis=1, keepdims=True) + jnp.sum(
        jnp.exp(lrecv[0] - top) + jnp.exp(lrecv[1] - top), axis=1, keepdims=True
    )

    def resp_copy(h, q, src_of):
        return remote(rall.at[h, src_of], rall.at[h, src_of], r_s.at[h, q], r_r.at[h, src_of], mate(q))

    for h in (1, 0):
        rall[h, pl.ds(me, 1)] = (weights[h] / totals).astype(bf16)[None]
        each(lambda q: resp_copy(h, q, me).start())
    column = top + jnp.log(totals)
    eye = lax.broadcasted_iota(jnp.int32, (nimg, nimg), 0) == lax.broadcasted_iota(
        jnp.int32, (nimg, nimg), 1
    )
    loglik[...] = jnp.sum(jnp.where(eye, column, 0.0), axis=0, keepdims=True)

    def near_copy(k, step):
        return remote(sums.at[POS[k]], rr.at[k], z_s.at[k], z_r.at[k], along(step))

    near = {dst: -step for src in RELAY for dst, step in RELAY[src]}

    for h in (1, 0):
        each(lambda q: resp_copy(h, q, q).wait_recv())
        resp = rall[h].reshape(plane * nimg, ntpl).astype(f32).T.astype(bf16)
        for c in range(2):
            res = lax.dot_general(
                resp,
                img_buf[c].reshape(plane * nimg, part),
                (((1,), (0,)), ((), ())),
                preferred_element_type=f32,
            )
            sums[h * half : (h + 1) * half, :, c * part : (c + 1) * part] = res.astype(bf16).reshape(
                half, plane, part
            )
            for k in (0, 4, 8, 12):
                i = POS[k] - h * half
                if 0 <= i < half:
                    own_sums[k // 4, :, c * part : (c + 1) * part] = res[i * plane : (i + 1) * plane]
        for k in ORDER[h * half : (h + 1) * half]:
            if k in near:
                near_copy(k, near[k]).start()

    def far_copy(j):
        return remote(r2_send.at[j], r2_recv.at[j], z2_s.at[j], z2_r.at[j], along(4 * j if j < 3 else -4))

    for j in (2, 1, 3, 0):
        val = own_sums[j]
        for k, step in RELAY[4 * j]:
            near_copy(k, near[k]).wait_recv()
            val = val + rr[k].astype(f32)
        if j > 0:
            r2_send[j] = val.astype(bf16)
            far_copy(j).start()
    for j in (1, 3, 2):
        far_copy(j).wait_recv()
        val = val + r2_recv[j].astype(f32)
    for k in range(tile_rows):
        fsend[pl.ds(k, plane, stride=tile_rows), :] = val[:, k * side : (k + 1) * side]

    def final_copy(q, src_of):
        return remote(fsend.at[rows_of(q)], fin.at[rows_of(src_of)], f_s.at[q], f_r.at[src_of], mate(q))

    each(lambda q: final_copy(q, me).start())
    fin[rows_of(me), :] = fsend[rows_of(me), :]
    each(lambda q: final_copy(q, q).wait_recv())
    whole = fin[...]
    squares = jnp.sum(jnp.sum(whole * whole, axis=0, keepdims=True), axis=1, keepdims=True)
    scaled = whole * lax.rsqrt(squares / (side * side) + 1e-06)
    for q in range(plane):
        for h in range(2):
            at = q * tile_rows + h * part_rows
            stage[h, q * part_rows : (q + 1) * part_rows, :] = scaled[at : at + part_rows, :]
    half_copy = remote(stage.at[1 - pix], orecv, o_s, o_r, twin)
    half_copy.start()
    out[pl.ds(pix, 1)] = stage[pl.ds(pix, 1)]

    each(lambda q: image_copy(q, me).wait_send())
    each(lambda q: swap(q, pix).wait_send(), 0, plane)
    each(lambda q: template_copy(q, me).wait_send())
    for m in moves:
        block(*m).wait_send()
    for h in range(2):
        each(lambda q: score_copy(h, q, me).wait_send())
        each(lambda q: resp_copy(h, q, me).wait_send())
        logit_copy(h).wait_send()
    for k in near:
        near_copy(k, near[k]).wait_send()
    for j in (1, 2, 3):
        far_copy(j).wait_send()
    each(lambda q: final_copy(q, me).wait_send())
    half_copy.wait_recv()
    out[pl.ds(1 - pix, 1)] = orecv[...][None]
    half_copy.wait_send()


def on_device(
    images,
    conformers,
    atom_types,
    type_amp,
    type_width,
    view_angles,
    template_conf,
    template_view,
    group_ids,
    group_prec,
):
    nimg, half_rows, side = images.shape
    plane = NX * NY
    part = half_rows * side // plane
    half = NZ // 2
    ntpl = half * plane
    parts = images.reshape(nimg, plane, part).transpose(1, 0, 2)
    bf16, f32 = jnp.bfloat16, jnp.float32
    vmem = pl.BlockSpec(memory_space=pltpu.VMEM)
    smem = pl.BlockSpec(memory_space=pltpu.SMEM)
    dma = pltpu.SemaphoreType.DMA
    natoms = atom_types.shape[0]
    averages, loglik = pl.pallas_call(
        functools.partial(em_kernel, side, min(512, natoms)),
        out_shape=(
            jax.ShapeDtypeStruct((2, half_rows, side), f32),
            jax.ShapeDtypeStruct((1, nimg), f32),
        ),
        in_specs=[smem] * 4 + [vmem] * 6,
        out_specs=(vmem, vmem),
        scratch_shapes=[
            pltpu.VMEM((2, plane, nimg, part), bf16),
            pltpu.VMEM((side, side), f32),
            pltpu.VMEM((side, side), f32),
            pltpu.VMEM((NZ, plane, 2 * part), bf16),
            pltpu.VMEM((2, plane, nimg + 8, ntpl), f32),
            pltpu.VMEM((2, plane, nimg + 8, ntpl), f32),
            pltpu.VMEM((2, nimg, ntpl), f32),
            pltpu.VMEM((2, nimg, ntpl), f32),
            pltpu.VMEM((2, plane, nimg, ntpl), bf16),
            pltpu.VMEM((4, plane, 2 * part), f32),
            pltpu.VMEM((NZ, plane, 2 * part), bf16),
            pltpu.VMEM((NZ, plane, 2 * part), bf16),
            pltpu.VMEM((4, plane, 2 * part), bf16),
            pltpu.VMEM((4, plane, 2 * part), bf16),
            pltpu.VMEM((side, side), f32),
            pltpu.VMEM((side, side), f32),
            pltpu.VMEM((2, half_rows, side), f32),
            pltpu.VMEM((half_rows, side), f32),
            pltpu.VMEM((side, side), f32),
            dma((plane,)),
            dma((plane,)),
            dma((plane,)),
            dma((plane,)),
            dma((plane,)),
            dma((plane,)),
            dma((NZ,)),
            dma((NZ,)),
            dma((2, plane)),
            dma((2, plane)),
            dma((2,)),
            dma((2,)),
            dma((2, plane)),
            dma((2, plane)),
            dma((NZ,)),
            dma((NZ,)),
            dma((4,)),
            dma((4,)),
            dma((plane,)),
            dma((plane,)),
            dma,
            dma,
            dma,
        ],
        compiler_params=pltpu.CompilerParams(
            collective_id=0, has_side_effects=True, vmem_limit_bytes=56 * 1024 * 1024
        ),
    )(
        template_conf,
        template_view,
        type_amp,
        type_width,
        parts,
        conformers,
        atom_types[None, :],
        view_angles,
        group_ids[None, :],
        group_prec[None, :],
    )
    return averages, loglik[0]


def solution(mesh):
    placed = (
        P(("img", "tpl"), "pix", None),
        P(),
        P(),
        P(),
        P(),
        P(),
        P(("tpl", "img")),
        P(("tpl", "img")),
        P("img"),
        P(),
    )
    return jax.shard_map(
        on_device,
        mesh=mesh,
        in_specs=placed,
        out_specs=(P(("tpl", "img"), "pix", None), P(("img", "tpl"))),
        check_vma=False,
    )
```

```python
import functools

import jax
import jax.numpy as jnp
from jax import lax
from jax.experimental import pallas as pl
from jax.experimental.pallas import tpu as pltpu
from jax.sharding import PartitionSpec as P

NX, NY, NZL = 4, 4, 4
MESH = pl.DeviceIdType.MESH
NT = (((1,), (1,)), ((), ()))


EARLY = (0, 1, 2, 3, 4, 12, 14, 15)
LATE = (8, 7, 9, 5, 6, 10, 11, 13)
ORDER = EARLY + LATE
POS = {k: i for i, k in enumerate(ORDER)}
NZ = 16
RELAY = {0: ((1, -1), (15, 1), (2, -2), (14, 2)), 4: ((5, -1), (3, 1), (6, -2)), 12: ((13, -1), (11, 1), (10, 2)), 8: ((9, -1), (7, 1))}
OWN_MOVES = ((0, 8, 8), (0, 12, 4), (0, 4, -4), (0, 3, -3), (0, 1, -1), (0, 15, 1), (0, 2, -2), (0, 14, 2))
RELAY_MOVES = {4: ((4, 5, -1), (4, 6, -2)), 12: ((12, 13, -1), (12, 11, 1), (12, 10, 2)), 8: ((8, 9, -1), (8, 7, 1))}
STEPS = (1, -1, 2, -2, 3, -3, 4, -4, 8)


def em_kernel(
    side,
    kc,
    conf_sm,
    view_sm,
    tamp_sm,
    twid_sm,
    images,
    conformers,
    types,
    angles,
    ids,
    group_prec,
    out,
    loglik,
    img_buf,
    tsend,
    tbuf,
    tall,
    ssend,
    srecv,
    lsend,
    lrecv,
    rall,
    own_sums,
    sums,
    rr,
    r2_send,
    r2_recv,
    fsend,
    fin,
    stage,
    orecv,
    acc,
    i_s,
    i_r,
    x_s,
    x_r,
    t_s,
    t_r,
    a_s,
    a_r,
    s_s,
    s_r,
    l_s,
    l_r,
    r_s,
    r_r,
    z_s,
    z_r,
    z2_s,
    z2_r,
    f_s,
    f_r,
    o_s,
    o_r,
    own_sem,
):
    f32, bf16 = jnp.float32, jnp.bfloat16
    plane = NX * NY
    img = lax.axis_index("img")
    tpl = lax.axis_index("tpl")
    pix = lax.axis_index("pix")
    x = lax.rem(img, NX)
    zl = lax.rem(lax.div(img, NX), NZL)
    y = lax.div(img, NX * NZL)
    z = tpl * NZL + zl
    me = y * NX + x
    half_rows = side // 2
    part_rows = half_rows // plane
    part = part_rows * side
    tile_rows = 2 * part_rows
    nimg = images.shape[1]
    half = len(EARLY)
    ntpl = half * plane
    full = 2 * part
    tile = 2 * tile_rows

    def mate(q):
        qy = lax.div(q, NX)
        qx = lax.rem(q, NX)
        return ((qy * NZL + zl) * NX + qx, tpl, pix)

    def along(step):
        zz = lax.rem(z + step + NZ, NZ)
        zt = lax.div(zz, NZL)
        zr = lax.rem(zz, NZL)
        return ((y * NZL + zr) * NX + x, zt, pix)

    twin = (img, tpl, 1 - pix)

    def rows_of(q):
        return pl.ds(pl.multiple_of(q * tile_rows, tile_rows), tile_rows)

    def tile_of(q):
        return pl.ds(pl.multiple_of(q * tile, tile), tile)

    def slot(q):
        return lax.rem(q, 2) * (plane // 2) + lax.div(q, 2)

    def remote(src, dst, ss, rs, dev):
        return pltpu.make_async_remote_copy(
            src_ref=src, dst_ref=dst, send_sem=ss, recv_sem=rs, device_id=dev, device_id_type=MESH
        )

    def each(body, first=1, last=plane, step=1):
        @pl.loop(first, last, step=step)
        def _(d):
            body(lax.rem(me + d, plane))

    bar = pltpu.get_barrier_semaphore()
    each(lambda q: pl.semaphore_signal(bar, inc=1, device_id=mate(q), device_id_type=MESH))
    for step in STEPS:
        pl.semaphore_signal(bar, inc=1, device_id=along(step), device_id_type=MESH)
    pl.semaphore_signal(bar, inc=1, device_id=twin, device_id_type=MESH)

    own = pltpu.make_async_copy(images.at[me], img_buf.at[pix, slot(me)], own_sem)
    own.start()

    conf = conf_sm[pix]
    view = angles[pl.ds(view_sm[pix], 1), :]
    cosines = jnp.cos(view)
    sines = jnp.sin(view)
    cos_phi, cos_theta, cos_psi = (cosines[:, i : i + 1] for i in range(3))
    sin_phi, sin_theta, sin_psi = (sines[:, i : i + 1] for i in range(3))
    r00 = cos_phi * cos_theta * cos_psi - sin_phi * sin_psi
    r01 = -cos_phi * cos_theta * sin_psi - sin_phi * cos_psi
    r02 = cos_phi * sin_theta
    r10 = sin_phi * cos_theta * cos_psi + cos_phi * sin_psi
    r11 = -sin_phi * cos_theta * sin_psi + cos_phi * cos_psi
    r12 = sin_phi * sin_theta
    s_idx = lax.broadcasted_iota(jnp.int32, (side, 1), 0)
    owner = s_idx // tile_rows
    in_tile = lax.rem(s_idx, tile_rows)
    row_id = (in_tile // part_rows) * half_rows + owner * part_rows + lax.rem(in_tile, part_rows)
    row_pos = row_id.astype(f32) - side * 0.5 + 0.5
    col_pos = s_idx.astype(f32) - side * 0.5 + 0.5
    acc[...] = jnp.zeros_like(acc)

    @pl.loop(0, types.shape[1] // kc)
    def _(k):
        sl = pl.ds(pl.multiple_of(k * kc, kc), kc)
        kind = types[:, sl]
        amp = jnp.zeros((1, kc), f32)
        width = jnp.zeros((1, kc), f32)
        for j in range(tamp_sm.shape[0]):
            amp = jnp.where(kind == j, tamp_sm[j], amp)
            width = jnp.where(kind == j, twid_sm[j], width)
        amp = amp * 0.0625
        spread = 0.5 / (width * width)
        c0 = conformers[conf, 0:1, sl]
        c1 = conformers[conf, 1:2, sl]
        c2 = conformers[conf, 2:3, sl]
        across = r00 * c0 + r01 * c1 + r02 * c2
        below = r10 * c0 + r11 * c1 + r12 * c2
        dc = col_pos - across
        dr = row_pos - below
        col = jnp.exp(-(dc * dc) * spread)
        row = amp * jnp.exp(-(dr * dr) * spread)
        col_hi = col.astype(bf16)
        col_lo = (col - col_hi.astype(f32)).astype(bf16)
        row_hi = row.astype(bf16)
        row_lo = (row - row_hi.astype(f32)).astype(bf16)
        total = lax.dot_general(row_hi, col_lo, NT, preferred_element_type=f32)
        total += lax.dot_general(row_lo, col_hi, NT, preferred_element_type=f32)
        total += lax.dot_general(row_hi, col_hi, NT, preferred_element_type=f32)
        acc[...] += total

    rendered = acc[...].astype(bf16).astype(f32)
    square = rendered * rendered
    norm = jnp.sum(jnp.sum(square, axis=0, keepdims=True), axis=1, keepdims=True)
    for q in range(plane):
        tsend[q * tile : q * tile + tile_rows, :] = rendered[q * tile_rows : (q + 1) * tile_rows, :]
        tsend[q * tile + tile_rows : (q + 1) * tile, :] = jnp.broadcast_to(norm, (tile_rows, side))

    groups = ids.shape[1]
    at_row = lax.broadcasted_iota(jnp.int32, (nimg, groups), 0)
    at_col = lax.broadcasted_iota(jnp.int32, (nimg, groups), 1)
    own_id = jnp.sum(
        jnp.where(at_col == at_row + tpl * nimg, ids[...].astype(f32), 0.0), axis=1, keepdims=True
    )
    ngrp = group_prec.shape[1]
    grp = lax.broadcasted_iota(jnp.int32, (nimg, ngrp), 1).astype(f32)
    prec = jnp.sum(jnp.where(grp == own_id, group_prec[...], 0.0), axis=1, keepdims=True)

    pl.semaphore_wait(bar, plane - 1 + len(STEPS) + 1)

    def template_copy(q, src_of):
        return remote(tsend.at[tile_of(q)], tbuf.at[tile_of(src_of)], t_s.at[q], t_r.at[src_of], mate(q))

    each(lambda q: template_copy(q, me).start())

    def image_copy(q, src_of):
        return remote(
            images.at[q], img_buf.at[pix, slot(src_of)], i_s.at[q], i_r.at[src_of], mate(q)
        )

    each(lambda q: image_copy(q, me).start(), 1, plane, 2)

    def swap(q, h):
        return remote(img_buf.at[h, slot(q)], img_buf.at[h, slot(q)], x_s.at[q], x_r.at[q], twin)

    own.wait()
    swap(me, pix).start()

    tbuf[tile_of(me), :] = tsend[tile_of(me), :]
    each(lambda q: template_copy(q, q).wait_recv())
    for k in range(tile_rows):
        tall[POS[0], :, k * side : (k + 1) * side] = tbuf[
            pl.ds(k, plane, stride=tile), :
        ].astype(bf16)
    norms = tbuf[pl.ds(tile_rows, plane, stride=tile), :]
    first = norms.astype(bf16).astype(f32)
    second = (norms - first).astype(bf16).astype(f32)
    third = norms - first - second
    lane = lax.broadcasted_iota(jnp.int32, (plane, side), 1)
    pieces = jnp.where(lane == 0, first, jnp.where(lane == 1, second, jnp.where(lane == 2, third, 0.0)))
    tall[POS[0], :, full:] = pieces.astype(bf16)

    def block(src, dst, step):
        return remote(tall.at[POS[src]], tall.at[POS[dst]], a_s.at[dst], a_r.at[dst], along(step))

    def arrived(dst):
        block(dst, dst, 0).wait_recv()

    def relay(k):
        arrived(k)
        for m in RELAY_MOVES[k]:
            block(*m).start()

    for m in OWN_MOVES:
        block(*m).start()
    each(lambda q: image_copy(q, me).start(), 2, plane, 2)

    def pass_image(q):
        image_copy(q, q).wait_recv()
        swap(q, pix).start()

    def score_copy(h, q, src_of):
        return remote(
            ssend.at[h, slot(q)], srecv.at[h, slot(src_of)], s_s.at[h, q], s_r.at[h, src_of], mate(q)
        )

    group = 4

    def score_part(h, odd):
        base = lax.rem(me + odd, 2) * (plane // 2)

        @pl.loop(0, plane // 2 // group)
        def _(g):
            at = pl.ds(base + g * group, group)
            res = jnp.zeros((group * nimg, ntpl), f32)
            for c in range(2):
                res += lax.dot_general(
                    img_buf[c, at].reshape(group * nimg, part),
                    tall[h * half : (h + 1) * half, :, c * part : (c + 1) * part].reshape(ntpl, part),
                    NT,
                    preferred_element_type=f32,
                )
            ssend[h, at] = res.reshape(group, nimg, ntpl)

        each(lambda q: score_copy(h, q, me).start(), 2 - odd, plane, 2)

    each(pass_image, 1, plane, 2)
    relay(4)
    relay(12)
    for k in EARLY:
        if k not in (0, 4, 12):
            arrived(k)
    each(lambda q: swap(q, 1 - pix).wait_recv(), 1, plane, 2)
    score_part(0, 1)
    relay(8)
    each(pass_image, 2, plane, 2)
    each(lambda q: swap(q, 1 - pix).wait_recv(), 0, plane, 2)
    score_part(0, 0)
    for k in LATE:
        if k != 8:
            arrived(k)
    score_part(1, 1)
    score_part(1, 0)
    for h in range(2):
        srecv[h, pl.ds(slot(me), 1)] = ssend[h, pl.ds(slot(me), 1)]

    def logit_copy(h):
        return remote(lsend.at[h], lrecv.at[h], l_s.at[h], l_r.at[h], twin)

    chosen = (lax.broadcasted_iota(jnp.int32, (8, side), 1) < 3).astype(f32).astype(bf16)
    for h in range(2):
        norm = lax.dot_general(
            chosen,
            tall[h * half : (h + 1) * half, :, full:].reshape(ntpl, side),
            NT,
            preferred_element_type=f32,
        )
        gain = prec * lax.rsqrt(norm[:1] + 1e-06)
        each(lambda q: score_copy(h, q, q).wait_recv())
        lsend[h] = gain * jnp.sum(srecv[h], axis=0)
        logit_copy(h).start()
    own_top = jnp.max(jnp.maximum(lsend[0], lsend[1]), axis=1, keepdims=True)
    for h in range(2):
        logit_copy(h).wait_recv()
    top = jnp.maximum(
        own_top, jnp.max(jnp.maximum(lrecv[0], lrecv[1]), axis=1, keepdims=True)
    )
    weights = [jnp.exp(lsend[h] - top) for h in range(2)]
    totals = jnp.sum(weights[0] + weights[1], axis=1, keepdims=True) + jnp.sum(
        jnp.exp(lrecv[0] - top) + jnp.exp(lrecv[1] - top), axis=1, keepdims=True
    )

    def resp_copy(h, q, src_of):
        return remote(
            rall.at[h, slot(src_of)], rall.at[h, slot(src_of)], r_s.at[h, q], r_r.at[h, src_of], mate(q)
        )

    for h in (1, 0):
        rall[h, pl.ds(slot(me), 1)] = (weights[h] / totals).astype(bf16)[None]
        each(lambda q: resp_copy(h, q, me).start())
    column = top + jnp.log(totals)
    eye = lax.broadcasted_iota(jnp.int32, (nimg, nimg), 0) == lax.broadcasted_iota(
        jnp.int32, (nimg, nimg), 1
    )
    loglik[...] = jnp.sum(jnp.where(eye, column, 0.0), axis=0, keepdims=True)

    def near_copy(k, step):
        return remote(sums.at[POS[k]], rr.at[k], z_s.at[k], z_r.at[k], along(step))

    near = {dst: -step for src in RELAY for dst, step in RELAY[src]}

    for h in (1, 0):
        each(lambda q: resp_copy(h, q, q).wait_recv())
        resp = rall[h].reshape(plane * nimg, ntpl).astype(f32).T.astype(bf16)
        for c in range(2):
            res = lax.dot_general(
                resp,
                img_buf[c].reshape(plane * nimg, part),
                (((1,), (0,)), ((), ())),
                preferred_element_type=f32,
            )
            sums[h * half : (h + 1) * half, :, c * part : (c + 1) * part] = res.astype(bf16).reshape(
                half, plane, part
            )
            for k in (0, 4, 8, 12):
                i = POS[k] - h * half
                if 0 <= i < half:
                    own_sums[k // 4, :, c * part : (c + 1) * part] = res[i * plane : (i + 1) * plane]
        for k in ORDER[h * half : (h + 1) * half]:
            if k in near:
                near_copy(k, near[k]).start()

    def far_copy(j):
        return remote(r2_send.at[j], r2_recv.at[j], z2_s.at[j], z2_r.at[j], along(4 * j if j < 3 else -4))

    for j in (2, 1, 3, 0):
        val = own_sums[j]
        for k, step in RELAY[4 * j]:
            near_copy(k, near[k]).wait_recv()
            val = val + rr[k].astype(f32)
        if j > 0:
            r2_send[j] = val.astype(bf16)
            far_copy(j).start()
    for j in (1, 3, 2):
        far_copy(j).wait_recv()
        val = val + r2_recv[j].astype(f32)
    for k in range(tile_rows):
        fsend[pl.ds(k, plane, stride=tile_rows), :] = val[:, k * side : (k + 1) * side]

    def final_copy(q, src_of):
        return remote(fsend.at[rows_of(q)], fin.at[rows_of(src_of)], f_s.at[q], f_r.at[src_of], mate(q))

    each(lambda q: final_copy(q, me).start())
    fin[rows_of(me), :] = fsend[rows_of(me), :]
    each(lambda q: final_copy(q, q).wait_recv())
    whole = fin[...]
    squares = jnp.sum(jnp.sum(whole * whole, axis=0, keepdims=True), axis=1, keepdims=True)
    scaled = whole * lax.rsqrt(squares / (side * side) + 1e-06)
    for q in range(plane):
        for h in range(2):
            at = q * tile_rows + h * part_rows
            stage[h, q * part_rows : (q + 1) * part_rows, :] = scaled[at : at + part_rows, :]
    half_copy = remote(stage.at[1 - pix], orecv, o_s, o_r, twin)
    half_copy.start()
    out[pl.ds(pix, 1)] = stage[pl.ds(pix, 1)]

    each(lambda q: image_copy(q, me).wait_send())
    each(lambda q: swap(q, pix).wait_send(), 0, plane)
    each(lambda q: template_copy(q, me).wait_send())
    for m in OWN_MOVES + RELAY_MOVES[4] + RELAY_MOVES[12] + RELAY_MOVES[8]:
        block(*m).wait_send()
    for h in range(2):
        each(lambda q: score_copy(h, q, me).wait_send())
        each(lambda q: resp_copy(h, q, me).wait_send())
        logit_copy(h).wait_send()
    for k in near:
        near_copy(k, near[k]).wait_send()
    for j in (1, 2, 3):
        far_copy(j).wait_send()
    each(lambda q: final_copy(q, me).wait_send())
    half_copy.wait_recv()
    out[pl.ds(1 - pix, 1)] = orecv[...][None]
    half_copy.wait_send()


def on_device(
    images,
    conformers,
    atom_types,
    type_amp,
    type_width,
    view_angles,
    template_conf,
    template_view,
    group_ids,
    group_prec,
):
    nimg, half_rows, side = images.shape
    plane = NX * NY
    part = half_rows * side // plane
    half = NZ // 2
    ntpl = half * plane
    parts = images.reshape(nimg, plane, part).transpose(1, 0, 2)
    bf16, f32 = jnp.bfloat16, jnp.float32
    vmem = pl.BlockSpec(memory_space=pltpu.VMEM)
    smem = pl.BlockSpec(memory_space=pltpu.SMEM)
    dma = pltpu.SemaphoreType.DMA
    natoms = atom_types.shape[0]
    averages, loglik = pl.pallas_call(
        functools.partial(em_kernel, side, min(512, natoms)),
        out_shape=(
            jax.ShapeDtypeStruct((2, half_rows, side), f32),
            jax.ShapeDtypeStruct((1, nimg), f32),
        ),
        in_specs=[smem] * 4 + [vmem] * 6,
        out_specs=(vmem, vmem),
        scratch_shapes=[
            pltpu.VMEM((2, plane, nimg, part), bf16),
            pltpu.VMEM((2 * side, side), f32),
            pltpu.VMEM((2 * side, side), f32),
            pltpu.VMEM((NZ, plane, 2 * part + side), bf16),
            pltpu.VMEM((2, plane, nimg, ntpl), f32),
            pltpu.VMEM((2, plane, nimg, ntpl), f32),
            pltpu.VMEM((2, nimg, ntpl), f32),
            pltpu.VMEM((2, nimg, ntpl), f32),
            pltpu.VMEM((2, plane, nimg, ntpl), bf16),
            pltpu.VMEM((4, plane, 2 * part), f32),
            pltpu.VMEM((NZ, plane, 2 * part), bf16),
            pltpu.VMEM((NZ, plane, 2 * part), bf16),
            pltpu.VMEM((4, plane, 2 * part), bf16),
            pltpu.VMEM((4, plane, 2 * part), bf16),
            pltpu.VMEM((side, side), f32),
            pltpu.VMEM((side, side), f32),
            pltpu.VMEM((2, half_rows, side), f32),
            pltpu.VMEM((half_rows, side), f32),
            pltpu.VMEM((side, side), f32),
            dma((plane,)),
            dma((plane,)),
            dma((plane,)),
            dma((plane,)),
            dma((plane,)),
            dma((plane,)),
            dma((NZ,)),
            dma((NZ,)),
            dma((2, plane)),
            dma((2, plane)),
            dma((2,)),
            dma((2,)),
            dma((2, plane)),
            dma((2, plane)),
            dma((NZ,)),
            dma((NZ,)),
            dma((4,)),
            dma((4,)),
            dma((plane,)),
            dma((plane,)),
            dma,
            dma,
            dma,
        ],
        compiler_params=pltpu.CompilerParams(
            collective_id=0, has_side_effects=True, vmem_limit_bytes=28 * 1024 * 1024
        ),
    )(
        template_conf,
        template_view,
        type_amp,
        type_width,
        parts,
        conformers,
        atom_types[None, :],
        view_angles,
        group_ids[None, :],
        group_prec[None, :],
    )
    return averages, loglik[0]


def solution(mesh):
    placed = (
        P(("img", "tpl"), "pix", None),
        P(),
        P(),
        P(),
        P(),
        P(),
        P(("tpl", "img")),
        P(("tpl", "img")),
        P("img"),
        P(),
    )
    return jax.shard_map(
        on_device,
        mesh=mesh,
        in_specs=placed,
        out_specs=(P(("tpl", "img"), "pix", None), P(("img", "tpl"))),
        check_vma=False,
    )
```

```python
import functools

import jax
import jax.numpy as jnp
from jax import lax
from jax.experimental import pallas as pl
from jax.experimental.pallas import tpu as pltpu
from jax.sharding import PartitionSpec as P

NX, NY, NZL = 4, 4, 4
MESH = pl.DeviceIdType.MESH
NT = (((1,), (1,)), ((), ()))


EARLY = (0, 1, 2, 5, 11, 13, 14, 15)
LATE = (8, 3, 7, 9, 4, 6, 10, 12)
ORDER = EARLY + LATE
POS = {k: i for i, k in enumerate(ORDER)}
NZ = 16
RELAY = {
    0: ((1, -1), (15, 1), (2, -2), (14, 2)),
    5: ((8, -3), (3, 2), (7, -2), (4, 1), (6, -1)),
    11: ((13, -2), (9, 2), (10, 1), (12, -1)),
}
FAR = {5: 5, 11: -5}
BASE = {k: i for i, k in enumerate(RELAY)}
OWN_MOVES = ((0, 11, 5), (0, 5, -5), (0, 13, 3), (0, 1, -1), (0, 15, 1), (0, 2, -2), (0, 14, 2))
RELAY_MOVES = {
    5: ((5, 8, -3), (5, 3, 2), (5, 7, -2), (5, 4, 1), (5, 6, -1)),
    11: ((11, 9, 2), (11, 10, 1), (11, 12, -1)),
}
STEPS = (1, -1, 2, -2, 3, -3, 5, -5)


def em_kernel(
    side,
    kc,
    conf_sm,
    view_sm,
    tamp_sm,
    twid_sm,
    images,
    conformers,
    types,
    angles,
    ids,
    group_prec,
    out,
    loglik,
    img_buf,
    tsend,
    tbuf,
    tall,
    ssend,
    srecv,
    lsend,
    lrecv,
    rall,
    own_sums,
    sums,
    rr,
    r2_send,
    r2_recv,
    fsend,
    fin,
    stage,
    orecv,
    acc,
    i_s,
    i_r,
    x_s,
    x_r,
    t_s,
    t_r,
    a_s,
    a_r,
    s_s,
    s_r,
    l_s,
    l_r,
    r_s,
    r_r,
    z_s,
    z_r,
    z2_s,
    z2_r,
    f_s,
    f_r,
    o_s,
    o_r,
    own_sem,
):
    f32, bf16 = jnp.float32, jnp.bfloat16
    plane = NX * NY
    img = lax.axis_index("img")
    tpl = lax.axis_index("tpl")
    pix = lax.axis_index("pix")
    x = lax.rem(img, NX)
    zl = lax.rem(lax.div(img, NX), NZL)
    y = lax.div(img, NX * NZL)
    z = tpl * NZL + zl
    me = y * NX + x
    half_rows = side // 2
    part_rows = half_rows // plane
    part = part_rows * side
    tile_rows = 2 * part_rows
    nimg = images.shape[0]
    half = len(EARLY)
    ntpl = half * plane
    full = 2 * part
    tile = 2 * tile_rows

    def mate(q):
        qy = lax.div(q, NX)
        qx = lax.rem(q, NX)
        return ((qy * NZL + zl) * NX + qx, tpl, pix)

    def along(step):
        zz = lax.rem(z + step + NZ, NZ)
        zt = lax.div(zz, NZL)
        zr = lax.rem(zz, NZL)
        return ((y * NZL + zr) * NX + x, zt, pix)

    twin = (img, tpl, 1 - pix)

    def rows_of(q):
        return pl.ds(pl.multiple_of(q * tile_rows, tile_rows), tile_rows)

    def tile_of(q):
        return pl.ds(pl.multiple_of(q * tile, tile), tile)

    def slot(q):
        return lax.rem(q, 2) * (plane // 2) + lax.div(q, 2)

    def remote(src, dst, ss, rs, dev):
        return pltpu.make_async_remote_copy(
            src_ref=src, dst_ref=dst, send_sem=ss, recv_sem=rs, device_id=dev, device_id_type=MESH
        )

    def each(body, first=1, last=plane, step=1):
        @pl.loop(first, last, step=step)
        def _(d):
            body(lax.rem(me + d, plane))

    bar = pltpu.get_barrier_semaphore()
    each(lambda q: pl.semaphore_signal(bar, inc=1, device_id=mate(q), device_id_type=MESH))
    for step in STEPS:
        pl.semaphore_signal(bar, inc=1, device_id=along(step), device_id_type=MESH)
    pl.semaphore_signal(bar, inc=1, device_id=twin, device_id_type=MESH)

    def image_part(q):
        return images.at[:, pl.ds(pl.multiple_of(q * part, part), part)]

    own = pltpu.make_async_copy(image_part(me), img_buf.at[pix, slot(me)], own_sem)
    own.start()

    conf = conf_sm[pix]
    views = lax.broadcasted_iota(jnp.int32, angles.shape, 1)
    view = jnp.sum(jnp.where(views == view_sm[pix], angles[...], 0.0), axis=1, keepdims=True)
    cosines = jnp.cos(view)
    sines = jnp.sin(view)
    cos_phi, cos_theta, cos_psi = (cosines[i : i + 1, :] for i in range(3))
    sin_phi, sin_theta, sin_psi = (sines[i : i + 1, :] for i in range(3))
    r00 = cos_phi * cos_theta * cos_psi - sin_phi * sin_psi
    r01 = -cos_phi * cos_theta * sin_psi - sin_phi * cos_psi
    r02 = cos_phi * sin_theta
    r10 = sin_phi * cos_theta * cos_psi + cos_phi * sin_psi
    r11 = -sin_phi * cos_theta * sin_psi + cos_phi * cos_psi
    r12 = sin_phi * sin_theta
    s_idx = lax.broadcasted_iota(jnp.int32, (side, 1), 0)
    owner = s_idx // tile_rows
    in_tile = lax.rem(s_idx, tile_rows)
    row_id = (in_tile // part_rows) * half_rows + owner * part_rows + lax.rem(in_tile, part_rows)
    row_pos = row_id.astype(f32) - side * 0.5 + 0.5
    col_pos = s_idx.astype(f32) - side * 0.5 + 0.5
    acc[...] = jnp.zeros_like(acc)

    @pl.loop(0, types.shape[1] // kc)
    def _(k):
        sl = pl.ds(pl.multiple_of(k * kc, kc), kc)
        kind = types[:, sl]
        amp = jnp.zeros((1, kc), f32)
        width = jnp.zeros((1, kc), f32)
        for j in range(tamp_sm.shape[0]):
            amp = jnp.where(kind == j, tamp_sm[j], amp)
            width = jnp.where(kind == j, twid_sm[j], width)
        amp = amp * 0.0625
        spread = 0.5 / (width * width)
        c0, c1, c2 = (conformers[i, pl.ds(conf, 1), sl] for i in range(3))
        across = r00 * c0 + r01 * c1 + r02 * c2
        below = r10 * c0 + r11 * c1 + r12 * c2
        dc = col_pos - across
        dr = row_pos - below
        col = jnp.exp(-(dc * dc) * spread)
        row = amp * jnp.exp(-(dr * dr) * spread)
        col_hi = col.astype(bf16)
        col_lo = (col - col_hi.astype(f32)).astype(bf16)
        row_hi = row.astype(bf16)
        row_lo = (row - row_hi.astype(f32)).astype(bf16)
        total = lax.dot_general(row_hi, col_lo, NT, preferred_element_type=f32)
        total += lax.dot_general(row_lo, col_hi, NT, preferred_element_type=f32)
        total += lax.dot_general(row_hi, col_hi, NT, preferred_element_type=f32)
        acc[...] += total

    rendered = acc[...].astype(bf16).astype(f32)
    square = rendered * rendered
    norm = jnp.sum(jnp.sum(square, axis=0, keepdims=True), axis=1, keepdims=True)
    for q in range(plane):
        tsend[q * tile : q * tile + tile_rows, :] = rendered[q * tile_rows : (q + 1) * tile_rows, :]
        tsend[q * tile + tile_rows : (q + 1) * tile, :] = jnp.broadcast_to(norm, (tile_rows, side))

    groups = ids.shape[1]
    at_row = lax.broadcasted_iota(jnp.int32, (nimg, groups), 0)
    at_col = lax.broadcasted_iota(jnp.int32, (nimg, groups), 1)
    own_id = jnp.sum(
        jnp.where(at_col == at_row + tpl * nimg, ids[...].astype(f32), 0.0), axis=1, keepdims=True
    )
    ngrp = group_prec.shape[1]
    grp = lax.broadcasted_iota(jnp.int32, (nimg, ngrp), 1).astype(f32)
    prec = jnp.sum(jnp.where(grp == own_id, group_prec[...], 0.0), axis=1, keepdims=True)

    pl.semaphore_wait(bar, plane - 1 + len(STEPS) + 1)

    def template_copy(q, src_of):
        return remote(tsend.at[tile_of(q)], tbuf.at[tile_of(src_of)], t_s.at[q], t_r.at[src_of], mate(q))

    each(lambda q: template_copy(q, me).start())

    def image_copy(q, src_of):
        return remote(
            image_part(q), img_buf.at[pix, slot(src_of)], i_s.at[q], i_r.at[src_of], mate(q)
        )

    each(lambda q: image_copy(q, me).start(), 1, plane, 2)

    def swap(q, h):
        return remote(img_buf.at[h, slot(q)], img_buf.at[h, slot(q)], x_s.at[q], x_r.at[q], twin)

    own.wait()
    swap(me, pix).start()

    tbuf[tile_of(me), :] = tsend[tile_of(me), :]
    each(lambda q: template_copy(q, q).wait_recv())
    for k in range(tile_rows):
        tall[POS[0], :, k * side : (k + 1) * side] = tbuf[
            pl.ds(k, plane, stride=tile), :
        ].astype(bf16)
    norms = tbuf[pl.ds(tile_rows, plane, stride=tile), :]
    first = norms.astype(bf16).astype(f32)
    second = (norms - first).astype(bf16).astype(f32)
    third = norms - first - second
    lane = lax.broadcasted_iota(jnp.int32, (plane, side), 1)
    pieces = jnp.where(lane == 0, first, jnp.where(lane == 1, second, jnp.where(lane == 2, third, 0.0)))
    tall[POS[0], :, full:] = pieces.astype(bf16)

    def block(src, dst, step):
        return remote(tall.at[POS[src]], tall.at[POS[dst]], a_s.at[dst], a_r.at[dst], along(step))

    def arrived(dst):
        block(dst, dst, 0).wait_recv()

    def relay(k):
        arrived(k)
        for m in RELAY_MOVES[k]:
            block(*m).start()

    for m in OWN_MOVES:
        block(*m).start()
    each(lambda q: image_copy(q, me).start(), 2, plane, 2)

    def pass_image(q):
        image_copy(q, q).wait_recv()
        swap(q, pix).start()

    def score_copy(h, q, src_of):
        return remote(
            ssend.at[h, slot(q)], srecv.at[h, slot(src_of)], s_s.at[h, q], s_r.at[h, src_of], mate(q)
        )

    group = 4

    def score_part(h, odd):
        base = lax.rem(me + odd, 2) * (plane // 2)

        @pl.loop(0, plane // 2 // group)
        def _(g):
            at = pl.ds(base + g * group, group)
            res = jnp.zeros((group * nimg, ntpl), f32)
            for c in range(2):
                res += lax.dot_general(
                    img_buf[c, at].reshape(group * nimg, part),
                    tall[h * half : (h + 1) * half, :, c * part : (c + 1) * part].reshape(ntpl, part),
                    NT,
                    preferred_element_type=f32,
                )
            ssend[h, at] = res.reshape(group, nimg, ntpl)

        each(lambda q: score_copy(h, q, me).start(), 2 - odd, plane, 2)

    each(pass_image, 1, plane, 2)
    relay(5)
    relay(11)
    for k in EARLY:
        if k not in BASE:
            arrived(k)
    each(lambda q: swap(q, 1 - pix).wait_recv(), 1, plane, 2)
    score_part(0, 1)
    each(pass_image, 2, plane, 2)
    each(lambda q: swap(q, 1 - pix).wait_recv(), 0, plane, 2)
    score_part(0, 0)
    for k in LATE:
        arrived(k)
    score_part(1, 1)
    score_part(1, 0)
    for h in range(2):
        srecv[h, pl.ds(slot(me), 1)] = ssend[h, pl.ds(slot(me), 1)]

    def logit_copy(h):
        return remote(lsend.at[h], lrecv.at[h], l_s.at[h], l_r.at[h], twin)

    chosen = (lax.broadcasted_iota(jnp.int32, (8, side), 1) < 3).astype(f32).astype(bf16)
    for h in range(2):
        norm = lax.dot_general(
            chosen,
            tall[h * half : (h + 1) * half, :, full:].reshape(ntpl, side),
            NT,
            preferred_element_type=f32,
        )
        gain = prec * lax.rsqrt(norm[:1] + 1e-06)
        each(lambda q: score_copy(h, q, q).wait_recv())
        lsend[h] = gain * jnp.sum(srecv[h], axis=0)
        logit_copy(h).start()
    own_top = jnp.max(jnp.maximum(lsend[0], lsend[1]), axis=1, keepdims=True)
    for h in range(2):
        logit_copy(h).wait_recv()
    top = jnp.maximum(
        own_top, jnp.max(jnp.maximum(lrecv[0], lrecv[1]), axis=1, keepdims=True)
    )
    weights = [jnp.exp(lsend[h] - top) for h in range(2)]
    totals = jnp.sum(weights[0] + weights[1], axis=1, keepdims=True) + jnp.sum(
        jnp.exp(lrecv[0] - top) + jnp.exp(lrecv[1] - top), axis=1, keepdims=True
    )

    def resp_copy(h, q, src_of):
        return remote(
            rall.at[h, slot(src_of)], rall.at[h, slot(src_of)], r_s.at[h, q], r_r.at[h, src_of], mate(q)
        )

    for h in (1, 0):
        rall[h, pl.ds(slot(me), 1)] = (weights[h] / totals).astype(bf16)[None]
        each(lambda q: resp_copy(h, q, me).start())
    column = top + jnp.log(totals)
    eye = lax.broadcasted_iota(jnp.int32, (nimg, nimg), 0) == lax.broadcasted_iota(
        jnp.int32, (nimg, nimg), 1
    )
    loglik[...] = jnp.sum(jnp.where(eye, column, 0.0), axis=0, keepdims=True)

    def near_copy(k, step):
        return remote(sums.at[POS[k]], rr.at[k], z_s.at[k], z_r.at[k], along(step))

    near = {dst: -step for src in RELAY for dst, step in RELAY[src]}

    def far_copy(b):
        j = BASE[b]
        return remote(r2_send.at[j], r2_recv.at[j], z2_s.at[j], z2_r.at[j], along(FAR[b]))

    def base_sum(b):
        val = own_sums[BASE[b]]
        for k, step in RELAY[b]:
            near_copy(k, near[k]).wait_recv()
            val = val + rr[k].astype(f32)
        return val

    def send_far(b):
        r2_send[BASE[b]] = base_sum(b).astype(bf16)
        far_copy(b).start()

    for h in (1, 0):
        each(lambda q: resp_copy(h, q, q).wait_recv())
        resp = rall[h].reshape(plane * nimg, ntpl).astype(f32).T.astype(bf16)
        for c in range(2):
            res = lax.dot_general(
                resp,
                img_buf[c].reshape(plane * nimg, part),
                (((1,), (0,)), ((), ())),
                preferred_element_type=f32,
            )
            sums[h * half : (h + 1) * half, :, c * part : (c + 1) * part] = res.astype(bf16).reshape(
                half, plane, part
            )
            for k in BASE:
                i = POS[k] - h * half
                if 0 <= i < half:
                    own_sums[BASE[k], :, c * part : (c + 1) * part] = res[i * plane : (i + 1) * plane]
        for k in (ORDER[half:] if h else (13, 2, 14, 1, 15)):
            if k in near:
                near_copy(k, near[k]).start()
    for b in FAR:
        send_far(b)
    val = base_sum(0)
    for b in FAR:
        far_copy(b).wait_recv()
        val = val + r2_recv[BASE[b]].astype(f32)
    for k in range(tile_rows):
        fsend[pl.ds(k, plane, stride=tile_rows), :] = val[:, k * side : (k + 1) * side]

    def final_copy(q, src_of):
        return remote(fsend.at[rows_of(q)], fin.at[rows_of(src_of)], f_s.at[q], f_r.at[src_of], mate(q))

    each(lambda q: final_copy(q, me).start())
    fin[rows_of(me), :] = fsend[rows_of(me), :]
    each(lambda q: final_copy(q, q).wait_recv())
    whole = fin[...]
    squares = jnp.sum(jnp.sum(whole * whole, axis=0, keepdims=True), axis=1, keepdims=True)
    scaled = whole * lax.rsqrt(squares / (side * side) + 1e-06)
    for q in range(plane):
        for h in range(2):
            at = q * tile_rows + h * part_rows
            stage[h, q * part_rows : (q + 1) * part_rows, :] = scaled[at : at + part_rows, :]
    half_copy = remote(stage.at[1 - pix], orecv, o_s, o_r, twin)
    half_copy.start()
    out[pl.ds(pix, 1)] = stage[pl.ds(pix, 1)]

    each(lambda q: image_copy(q, me).wait_send())
    each(lambda q: swap(q, pix).wait_send(), 0, plane)
    each(lambda q: template_copy(q, me).wait_send())
    for m in OWN_MOVES + RELAY_MOVES[5] + RELAY_MOVES[11]:
        block(*m).wait_send()
    for h in range(2):
        each(lambda q: score_copy(h, q, me).wait_send())
        each(lambda q: resp_copy(h, q, me).wait_send())
        logit_copy(h).wait_send()
    for k in near:
        near_copy(k, near[k]).wait_send()
    for b in FAR:
        far_copy(b).wait_send()
    each(lambda q: final_copy(q, me).wait_send())
    half_copy.wait_recv()
    out[pl.ds(1 - pix, 1)] = orecv[...][None]
    half_copy.wait_send()


def on_device(
    images,
    conformers,
    atom_types,
    type_amp,
    type_width,
    view_angles,
    template_conf,
    template_view,
    group_ids,
    group_prec,
):
    nimg, half_rows, side = images.shape
    plane = NX * NY
    part = half_rows * side // plane
    half = NZ // 2
    ntpl = half * plane
    flat = images.reshape(nimg, half_rows * side)
    bf16, f32 = jnp.bfloat16, jnp.float32
    vmem = pl.BlockSpec(memory_space=pltpu.VMEM)
    smem = pl.BlockSpec(memory_space=pltpu.SMEM)
    dma = pltpu.SemaphoreType.DMA
    natoms = atom_types.shape[0]
    averages, loglik = pl.pallas_call(
        functools.partial(em_kernel, side, min(512, natoms)),
        out_shape=(
            jax.ShapeDtypeStruct((2, half_rows, side), f32),
            jax.ShapeDtypeStruct((1, nimg), f32),
        ),
        in_specs=[smem] * 4 + [vmem] * 6,
        out_specs=(vmem, vmem),
        scratch_shapes=[
            pltpu.VMEM((2, plane, nimg, part), bf16),
            pltpu.VMEM((2 * side, side), f32),
            pltpu.VMEM((2 * side, side), f32),
            pltpu.VMEM((NZ, plane, 2 * part + side), bf16),
            pltpu.VMEM((2, plane, nimg, ntpl), f32),
            pltpu.VMEM((2, plane, nimg, ntpl), f32),
            pltpu.VMEM((2, nimg, ntpl), f32),
            pltpu.VMEM((2, nimg, ntpl), f32),
            pltpu.VMEM((2, plane, nimg, ntpl), bf16),
            pltpu.VMEM((len(RELAY), plane, 2 * part), f32),
            pltpu.VMEM((NZ, plane, 2 * part), bf16),
            pltpu.VMEM((NZ, plane, 2 * part), bf16),
            pltpu.VMEM((len(RELAY), plane, 2 * part), bf16),
            pltpu.VMEM((len(RELAY), plane, 2 * part), bf16),
            pltpu.VMEM((side, side), f32),
            pltpu.VMEM((side, side), f32),
            pltpu.VMEM((2, half_rows, side), f32),
            pltpu.VMEM((half_rows, side), f32),
            pltpu.VMEM((side, side), f32),
            dma((plane,)),
            dma((plane,)),
            dma((plane,)),
            dma((plane,)),
            dma((plane,)),
            dma((plane,)),
            dma((NZ,)),
            dma((NZ,)),
            dma((2, plane)),
            dma((2, plane)),
            dma((2,)),
            dma((2,)),
            dma((2, plane)),
            dma((2, plane)),
            dma((NZ,)),
            dma((NZ,)),
            dma((len(RELAY),)),
            dma((len(RELAY),)),
            dma((plane,)),
            dma((plane,)),
            dma,
            dma,
            dma,
        ],
        compiler_params=pltpu.CompilerParams(
            collective_id=0, has_side_effects=True, vmem_limit_bytes=28 * 1024 * 1024
        ),
    )(
        template_conf,
        template_view,
        type_amp,
        type_width,
        flat,
        conformers.transpose(1, 0, 2),
        atom_types[None, :],
        view_angles.T,
        group_ids[None, :],
        group_prec[None, :],
    )
    return averages, loglik[0]


def solution(mesh):
    placed = (
        P(("img", "tpl"), "pix", None),
        P(),
        P(),
        P(),
        P(),
        P(),
        P(("tpl", "img")),
        P(("tpl", "img")),
        P("img"),
        P(),
    )
    return jax.shard_map(
        on_device,
        mesh=mesh,
        in_specs=placed,
        out_specs=(P(("tpl", "img"), "pix", None), P(("img", "tpl"))),
        check_vma=False,
    )
```

```python
import functools

import jax
import jax.numpy as jnp
from jax import lax
from jax.experimental import pallas as pl
from jax.experimental.pallas import tpu as pltpu
from jax.sharding import PartitionSpec as P

NX, NY, NZL = 4, 4, 4
MESH = pl.DeviceIdType.MESH
NT = (((1,), (1,)), ((), ()))


EARLY = (0, 1, 2, 5, 11, 13, 14, 15)
LATE = (8, 3, 7, 9, 4, 6, 10, 12)
ORDER = EARLY + LATE
POS = {k: i for i, k in enumerate(ORDER)}
NZ = 16
RELAY = {
    0: ((1, -1), (15, 1), (2, -2), (14, 2)),
    5: ((8, -3), (3, 2), (7, -2), (4, 1), (6, -1)),
    11: ((13, -2), (9, 2), (10, 1), (12, -1)),
}
FAR = {5: 5, 11: -5}
BASE = {k: i for i, k in enumerate(RELAY)}
OWN_MOVES = ((0, 11, 5), (0, 5, -5), (0, 13, 3), (0, 1, -1), (0, 15, 1), (0, 2, -2), (0, 14, 2))
RELAY_MOVES = {
    5: ((5, 8, -3), (5, 3, 2), (5, 7, -2), (5, 4, 1), (5, 6, -1)),
    11: ((11, 9, 2), (11, 10, 1), (11, 12, -1)),
}
STEPS = (1, -1, 2, -2, 3, -3, 5, -5)


def em_kernel(
    side,
    kc,
    conf_sm,
    view_sm,
    tamp_sm,
    twid_sm,
    images,
    conformers,
    types,
    angles,
    ids,
    group_prec,
    out,
    loglik,
    img_buf,
    tsend,
    tbuf,
    tall,
    ssend,
    srecv,
    lsend,
    lrecv,
    rall,
    own_sums,
    sums,
    rr,
    r2_send,
    r2_recv,
    fsend,
    fin,
    stage,
    orecv,
    acc,
    i_s,
    i_r,
    x_s,
    x_r,
    t_s,
    t_r,
    a_s,
    a_r,
    s_s,
    s_r,
    l_s,
    l_r,
    r_s,
    r_r,
    z_s,
    z_r,
    z2_s,
    z2_r,
    f_s,
    f_r,
    o_s,
    o_r,
    own_sem,
):
    f32, bf16 = jnp.float32, jnp.bfloat16
    plane = NX * NY
    img = lax.axis_index("img")
    tpl = lax.axis_index("tpl")
    pix = lax.axis_index("pix")
    x = lax.rem(img, NX)
    zl = lax.rem(lax.div(img, NX), NZL)
    y = lax.div(img, NX * NZL)
    z = tpl * NZL + zl
    me = y * NX + x
    half_rows = side // 2
    part_rows = half_rows // plane
    part = part_rows * side
    tile_rows = 2 * part_rows
    nimg = images.shape[0]
    half = len(EARLY)
    ntpl = half * plane
    full = 2 * part
    tile = 2 * tile_rows

    def mate(q):
        qy = lax.div(q, NX)
        qx = lax.rem(q, NX)
        return ((qy * NZL + zl) * NX + qx, tpl, pix)

    def along(step):
        zz = lax.rem(z + step + NZ, NZ)
        zt = lax.div(zz, NZL)
        zr = lax.rem(zz, NZL)
        return ((y * NZL + zr) * NX + x, zt, pix)

    twin = (img, tpl, 1 - pix)

    def rows_of(q):
        return pl.ds(pl.multiple_of(q * tile_rows, tile_rows), tile_rows)

    def tile_of(q):
        return pl.ds(pl.multiple_of(q * tile, tile), tile)

    def slot(q):
        return lax.rem(q, 2) * (plane // 2) + lax.div(q, 2)

    def remote(src, dst, ss, rs, dev):
        return pltpu.make_async_remote_copy(
            src_ref=src, dst_ref=dst, send_sem=ss, recv_sem=rs, device_id=dev, device_id_type=MESH
        )

    def joint(src, dst, ss, rs):
        return remote(src, dst, ss, rs, twin)

    others = plane - 1

    def each(body, first=1, last=plane, step=1):
        @pl.loop(first, last, step=step)
        def _(d):
            body(lax.rem(me + d, plane))

    bar = pltpu.get_barrier_semaphore()
    each(lambda q: pl.semaphore_signal(bar, inc=1, device_id=mate(q), device_id_type=MESH))
    for step in STEPS:
        pl.semaphore_signal(bar, inc=1, device_id=along(step), device_id_type=MESH)
    pl.semaphore_signal(bar, inc=1, device_id=twin, device_id_type=MESH)

    def image_part(q):
        return images.at[:, pl.ds(pl.multiple_of(q * part, part), part)]

    own = pltpu.make_async_copy(image_part(me), img_buf.at[pix, slot(me)], own_sem)
    own.start()

    conf = conf_sm[pix]
    views = lax.broadcasted_iota(jnp.int32, angles.shape, 1)
    view = jnp.sum(jnp.where(views == view_sm[pix], angles[...], 0.0), axis=1, keepdims=True)
    cosines = jnp.cos(view)
    sines = jnp.sin(view)
    cos_phi, cos_theta, cos_psi = (cosines[i : i + 1, :] for i in range(3))
    sin_phi, sin_theta, sin_psi = (sines[i : i + 1, :] for i in range(3))
    r00 = cos_phi * cos_theta * cos_psi - sin_phi * sin_psi
    r01 = -cos_phi * cos_theta * sin_psi - sin_phi * cos_psi
    r02 = cos_phi * sin_theta
    r10 = sin_phi * cos_theta * cos_psi + cos_phi * sin_psi
    r11 = -sin_phi * cos_theta * sin_psi + cos_phi * cos_psi
    r12 = sin_phi * sin_theta
    s_idx = lax.broadcasted_iota(jnp.int32, (side, 1), 0)
    owner = s_idx // tile_rows
    in_tile = lax.rem(s_idx, tile_rows)
    row_id = (in_tile // part_rows) * half_rows + owner * part_rows + lax.rem(in_tile, part_rows)
    row_pos = row_id.astype(f32) - side * 0.5 + 0.5
    col_pos = s_idx.astype(f32) - side * 0.5 + 0.5
    acc[...] = jnp.zeros_like(acc)

    @pl.loop(0, types.shape[1] // kc)
    def _(k):
        sl = pl.ds(pl.multiple_of(k * kc, kc), kc)
        kind = types[:, sl]
        amp = jnp.zeros((1, kc), f32)
        width = jnp.zeros((1, kc), f32)
        for j in range(tamp_sm.shape[0]):
            amp = jnp.where(kind == j, tamp_sm[j], amp)
            width = jnp.where(kind == j, twid_sm[j], width)
        amp = amp * 0.0625
        spread = 0.5 / (width * width)
        c0, c1, c2 = (conformers[i, pl.ds(conf, 1), sl] for i in range(3))
        across = r00 * c0 + r01 * c1 + r02 * c2
        below = r10 * c0 + r11 * c1 + r12 * c2
        dc = col_pos - across
        dr = row_pos - below
        col = jnp.exp(-(dc * dc) * spread)
        row = amp * jnp.exp(-(dr * dr) * spread)
        col_hi = col.astype(bf16)
        col_lo = (col - col_hi.astype(f32)).astype(bf16)
        row_hi = row.astype(bf16)
        row_lo = (row - row_hi.astype(f32)).astype(bf16)
        total = lax.dot_general(row_hi, col_lo, NT, preferred_element_type=f32)
        total += lax.dot_general(row_lo, col_hi, NT, preferred_element_type=f32)
        total += lax.dot_general(row_hi, col_hi, NT, preferred_element_type=f32)
        acc[...] += total

    rendered = acc[...].astype(bf16).astype(f32)
    square = rendered * rendered
    norm = jnp.sum(jnp.sum(square, axis=0, keepdims=True), axis=1, keepdims=True)
    for q in range(plane):
        tsend[q * tile : q * tile + tile_rows, :] = rendered[q * tile_rows : (q + 1) * tile_rows, :]
        tsend[q * tile + tile_rows : (q + 1) * tile, :] = jnp.broadcast_to(norm, (tile_rows, side))

    groups = ids.shape[1]
    at_row = lax.broadcasted_iota(jnp.int32, (nimg, groups), 0)
    at_col = lax.broadcasted_iota(jnp.int32, (nimg, groups), 1)
    own_id = jnp.sum(
        jnp.where(at_col == at_row + tpl * nimg, ids[...].astype(f32), 0.0), axis=1, keepdims=True
    )
    ngrp = group_prec.shape[1]
    grp = lax.broadcasted_iota(jnp.int32, (nimg, ngrp), 1).astype(f32)
    prec = jnp.sum(jnp.where(grp == own_id, group_prec[...], 0.0), axis=1, keepdims=True)

    pl.semaphore_wait(bar, plane - 1 + len(STEPS) + 1)

    def template_copy(q):
        return remote(tsend.at[tile_of(q)], tbuf.at[tile_of(me)], t_s, t_r, mate(q))

    each(lambda q: template_copy(q).start())
    template_copies = joint(
        tsend.at[pl.ds(0, others * tile)], tbuf.at[pl.ds(0, others * tile)], t_s, t_r
    )

    def image_copy(q, g):
        return remote(image_part(q), img_buf.at[pix, slot(me)], i_s.at[g], i_r.at[g], mate(q))

    def image_copies(g):
        some = img_buf.at[pix, pl.ds(0, plane // 2 - 1 + g)]
        return joint(some, some, i_s.at[g], i_r.at[g])

    each(lambda q: image_copy(q, 1).start(), 1, plane, 2)

    def swap(g, h):
        some = img_buf.at[h, pl.ds(lax.rem(me + g, 2) * (plane // 2), plane // 2)]
        return remote(some, some, x_s.at[g], x_r.at[g], twin)

    tbuf[tile_of(me), :] = tsend[tile_of(me), :]
    template_copies.wait_recv()
    for k in range(tile_rows):
        tall[POS[0], :, k * side : (k + 1) * side] = tbuf[
            pl.ds(k, plane, stride=tile), :
        ].astype(bf16)
    norms = tbuf[pl.ds(tile_rows, plane, stride=tile), :]
    first = norms.astype(bf16).astype(f32)
    second = (norms - first).astype(bf16).astype(f32)
    third = norms - first - second
    lane = lax.broadcasted_iota(jnp.int32, (plane, side), 1)
    pieces = jnp.where(lane == 0, first, jnp.where(lane == 1, second, jnp.where(lane == 2, third, 0.0)))
    tall[POS[0], :, full:] = pieces.astype(bf16)

    def block(src, dst, step):
        way = 3 if dst in LATE else BASE.get(dst, 0)
        return remote(tall.at[POS[src]], tall.at[POS[dst]], a_s, a_r.at[way], along(step))

    def blocks(count, way):
        return joint(tall.at[pl.ds(0, count)], tall.at[pl.ds(0, count)], a_s, a_r.at[way])

    def relay(k):
        blocks(1, BASE[k]).wait_recv()
        for m in RELAY_MOVES[k]:
            block(*m).start()

    for m in OWN_MOVES:
        block(*m).start()
    each(lambda q: image_copy(q, 0).start(), 2, plane, 2)

    def score_copy(h, q, src_of):
        return remote(
            ssend.at[h, slot(q)], srecv.at[h, slot(src_of)], s_s.at[h], s_r.at[h], mate(q)
        )

    def score_copies(h):
        return joint(
            ssend.at[h, pl.ds(0, others)], srecv.at[h, pl.ds(0, others)], s_s.at[h], s_r.at[h]
        )

    group = 4

    def score_part(h, odd):
        base = lax.rem(me + odd, 2) * (plane // 2)

        @pl.loop(0, plane // 2 // group)
        def _(g):
            at = pl.ds(base + g * group, group)
            res = jnp.zeros((group * nimg, ntpl), f32)
            for c in range(2):
                res += lax.dot_general(
                    img_buf[c, at].reshape(group * nimg, part),
                    tall[h * half : (h + 1) * half, :, c * part : (c + 1) * part].reshape(ntpl, part),
                    NT,
                    preferred_element_type=f32,
                )
            ssend[h, at] = res.reshape(group, nimg, ntpl)

        each(lambda q: score_copy(h, q, me).start(), 2 - odd, plane, 2)

    image_copies(1).wait_recv()
    swap(1, pix).start()
    relay(5)
    relay(11)
    blocks(len(EARLY) - len(BASE), 0).wait_recv()
    swap(1, 1 - pix).wait_recv()
    score_part(0, 1)
    image_copies(0).wait_recv()
    own.wait()
    swap(0, pix).start()
    swap(0, 1 - pix).wait_recv()
    score_part(0, 0)
    blocks(len(LATE), 3).wait_recv()
    score_part(1, 1)
    score_part(1, 0)
    template_copies.wait_send()
    for g in range(2):
        image_copies(g).wait_send()
        swap(g, pix).wait_send()
    blocks(NZ - 1, 0).wait_send()
    for h in range(2):
        srecv[h, pl.ds(slot(me), 1)] = ssend[h, pl.ds(slot(me), 1)]

    def logit_copy(h):
        return remote(lsend.at[h], lrecv.at[h], l_s.at[h], l_r.at[h], twin)

    chosen = (lax.broadcasted_iota(jnp.int32, (8, side), 1) < 3).astype(f32).astype(bf16)
    for h in range(2):
        norm = lax.dot_general(
            chosen,
            tall[h * half : (h + 1) * half, :, full:].reshape(ntpl, side),
            NT,
            preferred_element_type=f32,
        )
        gain = prec * lax.rsqrt(norm[:1] + 1e-06)
        score_copies(h).wait_recv()
        lsend[h] = gain * jnp.sum(srecv[h], axis=0)
        logit_copy(h).start()
    own_top = jnp.max(jnp.maximum(lsend[0], lsend[1]), axis=1, keepdims=True)
    for h in range(2):
        logit_copy(h).wait_recv()
    top = jnp.maximum(
        own_top, jnp.max(jnp.maximum(lrecv[0], lrecv[1]), axis=1, keepdims=True)
    )
    weights = [jnp.exp(lsend[h] - top) for h in range(2)]
    totals = jnp.sum(weights[0] + weights[1], axis=1, keepdims=True) + jnp.sum(
        jnp.exp(lrecv[0] - top) + jnp.exp(lrecv[1] - top), axis=1, keepdims=True
    )

    def resp_copy(h, q):
        mine = rall.at[h, slot(me)]
        return remote(mine, mine, r_s.at[h], r_r.at[h], mate(q))

    def resp_copies(h):
        some = rall.at[h, pl.ds(0, others)]
        return joint(some, some, r_s.at[h], r_r.at[h])

    for h in (1, 0):
        rall[h, pl.ds(slot(me), 1)] = (weights[h] / totals).astype(bf16)[None]
        each(lambda q: resp_copy(h, q).start())
    column = top + jnp.log(totals)
    eye = lax.broadcasted_iota(jnp.int32, (nimg, nimg), 0) == lax.broadcasted_iota(
        jnp.int32, (nimg, nimg), 1
    )
    loglik[...] = jnp.sum(jnp.where(eye, column, 0.0), axis=0, keepdims=True)

    for h in range(2):
        score_copies(h).wait_send()
        logit_copy(h).wait_send()

    near = {dst: (base, -step) for base in RELAY for dst, step in RELAY[base]}

    def near_copy(k):
        base, step = near[k]
        return remote(sums.at[POS[k]], rr.at[k], z_s, z_r.at[BASE[base]], along(step))

    def near_copies(count, base):
        return joint(sums.at[pl.ds(0, count)], rr.at[pl.ds(0, count)], z_s, z_r.at[BASE[base]])

    def far_copy(b):
        j = BASE[b]
        return remote(r2_send.at[j], r2_recv.at[j], z2_s.at[j], z2_r.at[j], along(FAR[b]))

    def base_sum(b):
        val = own_sums[BASE[b]]
        near_copies(len(RELAY[b]), b).wait_recv()
        for k, step in RELAY[b]:
            val = val + rr[k].astype(f32)
        return val

    def send_far(b):
        r2_send[BASE[b]] = base_sum(b).astype(bf16)
        far_copy(b).start()

    for h in (1, 0):
        resp_copies(h).wait_recv()
        resp = rall[h].reshape(plane * nimg, ntpl).astype(f32).T.astype(bf16)
        for c in range(2):
            res = lax.dot_general(
                resp,
                img_buf[c].reshape(plane * nimg, part),
                (((1,), (0,)), ((), ())),
                preferred_element_type=f32,
            )
            sums[h * half : (h + 1) * half, :, c * part : (c + 1) * part] = res.astype(bf16).reshape(
                half, plane, part
            )
            for k in BASE:
                i = POS[k] - h * half
                if 0 <= i < half:
                    own_sums[BASE[k], :, c * part : (c + 1) * part] = res[i * plane : (i + 1) * plane]
        for k in (ORDER[half:] if h else (13, 2, 14, 1, 15)):
            if k in near:
                near_copy(k).start()
    for h in range(2):
        resp_copies(h).wait_send()
    for b in FAR:
        send_far(b)
    val = base_sum(0)
    for b in FAR:
        far_copy(b).wait_recv()
        val = val + r2_recv[BASE[b]].astype(f32)
    for k in range(tile_rows):
        fsend[pl.ds(k, plane, stride=tile_rows), :] = val[:, k * side : (k + 1) * side]

    def final_copy(q):
        return remote(fsend.at[rows_of(q)], fin.at[rows_of(me)], f_s, f_r, mate(q))

    each(lambda q: final_copy(q).start())
    final_copies = joint(
        fsend.at[pl.ds(0, others * tile_rows)], fin.at[pl.ds(0, others * tile_rows)], f_s, f_r
    )
    fin[rows_of(me), :] = fsend[rows_of(me), :]
    near_copies(len(near), 0).wait_send()
    for b in FAR:
        far_copy(b).wait_send()
    final_copies.wait_recv()
    whole = fin[...]
    squares = jnp.sum(jnp.sum(whole * whole, axis=0, keepdims=True), axis=1, keepdims=True)
    scaled = whole * lax.rsqrt(squares / (side * side) + 1e-06)
    for q in range(plane):
        for h in range(2):
            at = q * tile_rows + h * part_rows
            stage[h, q * part_rows : (q + 1) * part_rows, :] = scaled[at : at + part_rows, :]
    half_copy = remote(stage.at[1 - pix], orecv, o_s, o_r, twin)
    half_copy.start()
    out[pl.ds(pix, 1)] = stage[pl.ds(pix, 1)]

    final_copies.wait_send()
    half_copy.wait_recv()
    out[pl.ds(1 - pix, 1)] = orecv[...][None]
    half_copy.wait_send()


def on_device(
    images,
    conformers,
    atom_types,
    type_amp,
    type_width,
    view_angles,
    template_conf,
    template_view,
    group_ids,
    group_prec,
):
    nimg, half_rows, side = images.shape
    plane = NX * NY
    part = half_rows * side // plane
    half = NZ // 2
    ntpl = half * plane
    flat = images.reshape(nimg, half_rows * side)
    bf16, f32 = jnp.bfloat16, jnp.float32
    vmem = pl.BlockSpec(memory_space=pltpu.VMEM)
    smem = pl.BlockSpec(memory_space=pltpu.SMEM)
    dma = pltpu.SemaphoreType.DMA
    natoms = atom_types.shape[0]
    averages, loglik = pl.pallas_call(
        functools.partial(em_kernel, side, min(512, natoms)),
        out_shape=(
            jax.ShapeDtypeStruct((2, half_rows, side), f32),
            jax.ShapeDtypeStruct((1, nimg), f32),
        ),
        in_specs=[smem] * 4 + [vmem] * 6,
        out_specs=(vmem, vmem),
        scratch_shapes=[
            pltpu.VMEM((2, plane, nimg, part), bf16),
            pltpu.VMEM((2 * side, side), f32),
            pltpu.VMEM((2 * side, side), f32),
            pltpu.VMEM((NZ, plane, 2 * part + side), bf16),
            pltpu.VMEM((2, plane, nimg, ntpl), f32),
            pltpu.VMEM((2, plane, nimg, ntpl), f32),
            pltpu.VMEM((2, nimg, ntpl), f32),
            pltpu.VMEM((2, nimg, ntpl), f32),
            pltpu.VMEM((2, plane, nimg, ntpl), bf16),
            pltpu.VMEM((len(RELAY), plane, 2 * part), f32),
            pltpu.VMEM((NZ, plane, 2 * part), bf16),
            pltpu.VMEM((NZ, plane, 2 * part), bf16),
            pltpu.VMEM((len(RELAY), plane, 2 * part), bf16),
            pltpu.VMEM((len(RELAY), plane, 2 * part), bf16),
            pltpu.VMEM((side, side), f32),
            pltpu.VMEM((side, side), f32),
            pltpu.VMEM((2, half_rows, side), f32),
            pltpu.VMEM((half_rows, side), f32),
            pltpu.VMEM((side, side), f32),
            dma((2,)),
            dma((2,)),
            dma((2,)),
            dma((2,)),
            dma,
            dma,
            dma,
            dma((4,)),
            dma((2,)),
            dma((2,)),
            dma((2,)),
            dma((2,)),
            dma((2,)),
            dma((2,)),
            dma,
            dma((len(RELAY),)),
            dma((len(RELAY),)),
            dma((len(RELAY),)),
            dma,
            dma,
            dma,
            dma,
            dma,
        ],
        compiler_params=pltpu.CompilerParams(
            collective_id=0, has_side_effects=True, vmem_limit_bytes=28 * 1024 * 1024
        ),
    )(
        template_conf,
        template_view,
        type_amp,
        type_width,
        flat,
        conformers.transpose(1, 0, 2),
        atom_types[None, :],
        view_angles.T,
        group_ids[None, :],
        group_prec[None, :],
    )
    return averages, loglik[0]


def solution(mesh):
    placed = (
        P(("img", "tpl"), "pix", None),
        P(),
        P(),
        P(),
        P(),
        P(),
        P(("tpl", "img")),
        P(("tpl", "img")),
        P("img"),
        P(),
    )
    return jax.shard_map(
        on_device,
        mesh=mesh,
        in_specs=placed,
        out_specs=(P(("tpl", "img"), "pix", None), P(("img", "tpl"))),
        check_vma=False,
    )
```

```python
import functools

import jax
import jax.numpy as jnp
from jax import lax
from jax.experimental import pallas as pl
from jax.experimental.pallas import tpu as pltpu
from jax.sharding import PartitionSpec as P

NX, NY, NZL = 4, 4, 4
MESH = pl.DeviceIdType.MESH
NT = (((1,), (1,)), ((), ()))


EARLY = (0, 1, 2, 5, 11, 13, 14, 15)
LATE = (8, 3, 7, 9, 4, 6, 10, 12)
ORDER = EARLY + LATE
POS = {k: i for i, k in enumerate(ORDER)}
NZ = 16
RELAY = {
    0: ((1, -1), (15, 1), (2, -2), (14, 2)),
    5: ((8, -3), (3, 2), (7, -2), (4, 1), (6, -1)),
    11: ((13, -2), (9, 2), (10, 1), (12, -1)),
}
FAR = {5: 5, 11: -5}
BASE = {k: i for i, k in enumerate(RELAY)}
OWN_MOVES = ((0, 11, 5), (0, 5, -5), (0, 13, 3), (0, 1, -1), (0, 15, 1), (0, 2, -2), (0, 14, 2))
RELAY_MOVES = {
    5: ((5, 8, -3), (5, 3, 2), (5, 7, -2), (5, 4, 1), (5, 6, -1)),
    11: ((11, 9, 2), (11, 10, 1), (11, 12, -1)),
}
STEPS = (1, -1, 2, -2, 3, -3, 5, -5)


def em_kernel(
    side,
    kc,
    conf_sm,
    view_sm,
    tamp_sm,
    twid_sm,
    images,
    conformers,
    types,
    angles,
    ids,
    group_prec,
    out,
    loglik,
    img_buf,
    tsend,
    tbuf,
    tall,
    ssend,
    srecv,
    lsend,
    lrecv,
    rall,
    own_sums,
    sums,
    rr,
    r2_send,
    r2_recv,
    fsend,
    fin,
    stage,
    orecv,
    acc,
    i_s,
    i_r,
    x_s,
    x_r,
    t_s,
    t_r,
    a_s,
    a_r,
    s_s,
    s_r,
    l_s,
    l_r,
    r_s,
    r_r,
    z_s,
    z_r,
    z2_s,
    z2_r,
    f_s,
    f_r,
    o_s,
    o_r,
    own_sem,
):
    f32, bf16 = jnp.float32, jnp.bfloat16
    plane = NX * NY
    img = lax.axis_index("img")
    tpl = lax.axis_index("tpl")
    pix = lax.axis_index("pix")
    x = lax.rem(img, NX)
    zl = lax.rem(lax.div(img, NX), NZL)
    y = lax.div(img, NX * NZL)
    z = tpl * NZL + zl
    me = y * NX + x
    half_rows = side // 2
    part_rows = half_rows // plane
    part = part_rows * side
    tile_rows = 2 * part_rows
    nimg = images.shape[0]
    half = len(EARLY)
    ntpl = half * plane
    full = 2 * part
    tile = 2 * tile_rows

    def mate(q):
        qy = lax.div(q, NX)
        qx = lax.rem(q, NX)
        return ((qy * NZL + zl) * NX + qx, tpl, pix)

    def along(step):
        zz = lax.rem(z + step + NZ, NZ)
        zt = lax.div(zz, NZL)
        zr = lax.rem(zz, NZL)
        return ((y * NZL + zr) * NX + x, zt, pix)

    twin = (img, tpl, 1 - pix)

    def rows_of(q):
        return pl.ds(pl.multiple_of(q * tile_rows, tile_rows), tile_rows)

    def tile_of(q):
        return pl.ds(pl.multiple_of(q * tile, tile), tile)

    def slot(q):
        return lax.rem(q, 2) * (plane // 2) + lax.div(q, 2)

    def remote(src, dst, ss, rs, dev):
        return pltpu.make_async_remote_copy(
            src_ref=src, dst_ref=dst, send_sem=ss, recv_sem=rs, device_id=dev, device_id_type=MESH
        )

    def joint(src, dst, ss, rs):
        return remote(src, dst, ss, rs, twin)

    others = plane - 1

    def each(body, first=1, last=plane, step=1):
        @pl.loop(first, last, step=step)
        def _(d):
            body(lax.rem(me + d, plane))

    bar = pltpu.get_barrier_semaphore()
    each(lambda q: pl.semaphore_signal(bar, inc=1, device_id=mate(q), device_id_type=MESH))
    for step in STEPS:
        pl.semaphore_signal(bar, inc=1, device_id=along(step), device_id_type=MESH)
    pl.semaphore_signal(bar, inc=1, device_id=twin, device_id_type=MESH)

    def image_part(q):
        return images.at[:, pl.ds(pl.multiple_of(q * part, part), part)]

    own = pltpu.make_async_copy(image_part(me), img_buf.at[pix, slot(me)], own_sem)
    own.start()

    conf = conf_sm[pix]
    views = lax.broadcasted_iota(jnp.int32, angles.shape, 1)
    view = jnp.sum(jnp.where(views == view_sm[pix], angles[...], 0.0), axis=1, keepdims=True)
    cosines = jnp.cos(view)
    sines = jnp.sin(view)
    cos_phi, cos_theta, cos_psi = (cosines[i : i + 1, :] for i in range(3))
    sin_phi, sin_theta, sin_psi = (sines[i : i + 1, :] for i in range(3))
    r00 = cos_phi * cos_theta * cos_psi - sin_phi * sin_psi
    r01 = -cos_phi * cos_theta * sin_psi - sin_phi * cos_psi
    r02 = cos_phi * sin_theta
    r10 = sin_phi * cos_theta * cos_psi + cos_phi * sin_psi
    r11 = -sin_phi * cos_theta * sin_psi + cos_phi * cos_psi
    r12 = sin_phi * sin_theta
    s_idx = lax.broadcasted_iota(jnp.int32, (side, 1), 0)
    owner = s_idx // tile_rows
    in_tile = lax.rem(s_idx, tile_rows)
    row_id = (in_tile // part_rows) * half_rows + owner * part_rows + lax.rem(in_tile, part_rows)
    row_pos = row_id.astype(f32) - side * 0.5 + 0.5
    col_pos = s_idx.astype(f32) - side * 0.5 + 0.5
    acc[...] = jnp.zeros_like(acc)

    @pl.loop(0, types.shape[1] // kc)
    def _(k):
        sl = pl.ds(pl.multiple_of(k * kc, kc), kc)
        kind = types[:, sl]
        amp = jnp.zeros((1, kc), f32)
        width = jnp.zeros((1, kc), f32)
        for j in range(tamp_sm.shape[0]):
            amp = jnp.where(kind == j, tamp_sm[j], amp)
            width = jnp.where(kind == j, twid_sm[j], width)
        amp = amp * 0.0625
        spread = 0.5 / (width * width)
        c0, c1, c2 = (conformers[i, pl.ds(conf, 1), sl] for i in range(3))
        across = r00 * c0 + r01 * c1 + r02 * c2
        below = r10 * c0 + r11 * c1 + r12 * c2
        dc = col_pos - across
        dr = row_pos - below
        col = jnp.exp(-(dc * dc) * spread)
        row = amp * jnp.exp(-(dr * dr) * spread)
        col_hi = col.astype(bf16)
        col_lo = (col - col_hi.astype(f32)).astype(bf16)
        row_hi = row.astype(bf16)
        row_lo = (row - row_hi.astype(f32)).astype(bf16)
        total = lax.dot_general(row_hi, col_lo, NT, preferred_element_type=f32)
        total += lax.dot_general(row_lo, col_hi, NT, preferred_element_type=f32)
        total += lax.dot_general(row_hi, col_hi, NT, preferred_element_type=f32)
        acc[...] += total

    rendered = acc[...].astype(bf16).astype(f32)
    square = rendered * rendered
    norm = jnp.sum(jnp.sum(square, axis=0, keepdims=True), axis=1, keepdims=True)
    for q in range(plane):
        tsend[q * tile : q * tile + tile_rows, :] = rendered[q * tile_rows : (q + 1) * tile_rows, :]
        tsend[q * tile + tile_rows : (q + 1) * tile, :] = jnp.broadcast_to(norm, (tile_rows, side))

    groups = ids.shape[1]
    at_row = lax.broadcasted_iota(jnp.int32, (nimg, groups), 0)
    at_col = lax.broadcasted_iota(jnp.int32, (nimg, groups), 1)
    own_id = jnp.sum(
        jnp.where(at_col == at_row + tpl * nimg, ids[...].astype(f32), 0.0), axis=1, keepdims=True
    )
    ngrp = group_prec.shape[1]
    grp = lax.broadcasted_iota(jnp.int32, (nimg, ngrp), 1).astype(f32)
    prec = jnp.sum(jnp.where(grp == own_id, group_prec[...], 0.0), axis=1, keepdims=True)

    pl.semaphore_wait(bar, plane - 1 + len(STEPS) + 1)

    def template_copy(q):
        return remote(tsend.at[tile_of(q)], tbuf.at[tile_of(me)], t_s, t_r, mate(q))

    each(lambda q: template_copy(q).start())
    template_copies = joint(
        tsend.at[pl.ds(0, others * tile)], tbuf.at[pl.ds(0, others * tile)], t_s, t_r
    )

    def image_copy(q, g):
        return remote(image_part(q), img_buf.at[pix, slot(me)], i_s.at[g], i_r.at[g], mate(q))

    def image_copies(g):
        some = img_buf.at[pix, pl.ds(0, plane // 2 - 1 + g)]
        return joint(some, some, i_s.at[g], i_r.at[g])

    each(lambda q: image_copy(q, 1).start(), 1, plane, 2)

    def swap(g, h):
        some = img_buf.at[h, pl.ds(lax.rem(me + g, 2) * (plane // 2), plane // 2)]
        return remote(some, some, x_s.at[g], x_r.at[g], twin)

    tbuf[tile_of(me), :] = tsend[tile_of(me), :]
    template_copies.wait_recv()
    for k in range(tile_rows):
        tall[POS[0], :, k * side : (k + 1) * side] = tbuf[
            pl.ds(k, plane, stride=tile), :
        ].astype(bf16)
    norms = tbuf[pl.ds(tile_rows, plane, stride=tile), :]
    first = norms.astype(bf16).astype(f32)
    second = (norms - first).astype(bf16).astype(f32)
    third = norms - first - second
    lane = lax.broadcasted_iota(jnp.int32, (plane, side), 1)
    pieces = jnp.where(lane == 0, first, jnp.where(lane == 1, second, jnp.where(lane == 2, third, 0.0)))
    tall[POS[0], :, full:] = pieces.astype(bf16)

    def block(src, dst, step):
        way = 3 if dst in LATE else BASE.get(dst, 0)
        return remote(tall.at[POS[src]], tall.at[POS[dst]], a_s, a_r.at[way], along(step))

    def blocks(count, way):
        return joint(tall.at[pl.ds(0, count)], tall.at[pl.ds(0, count)], a_s, a_r.at[way])

    def relay(k):
        blocks(1, BASE[k]).wait_recv()
        for m in RELAY_MOVES[k]:
            block(*m).start()

    for m in OWN_MOVES:
        block(*m).start()
    each(lambda q: image_copy(q, 0).start(), 2, plane, 2)

    def score_copy(h, q, src_of):
        return remote(
            ssend.at[h, slot(q)], srecv.at[h, slot(src_of)], s_s.at[h], s_r.at[h], mate(q)
        )

    def score_copies(h):
        return joint(
            ssend.at[h, pl.ds(0, others)], srecv.at[h, pl.ds(0, others)], s_s.at[h], s_r.at[h]
        )

    group = 8

    def score_part(h, odd):
        base = lax.rem(me + odd, 2) * (plane // 2)

        @pl.loop(0, plane // 2 // group)
        def _(g):
            at = pl.ds(base + g * group, group)
            res = jnp.zeros((group * nimg, ntpl), f32)
            for c in range(2):
                res += lax.dot_general(
                    img_buf[c, at].reshape(group * nimg, part),
                    tall[h * half : (h + 1) * half, :, c * part : (c + 1) * part].reshape(ntpl, part),
                    NT,
                    preferred_element_type=f32,
                )
            ssend[h, at] = res.reshape(group, nimg, ntpl)

        each(lambda q: score_copy(h, q, me).start(), 2 - odd, plane, 2)

    image_copies(1).wait_recv()
    swap(1, pix).start()
    relay(5)
    relay(11)
    blocks(len(EARLY) - len(BASE), 0).wait_recv()
    swap(1, 1 - pix).wait_recv()
    score_part(0, 1)
    image_copies(0).wait_recv()
    own.wait()
    swap(0, pix).start()
    swap(0, 1 - pix).wait_recv()
    score_part(0, 0)
    blocks(len(LATE), 3).wait_recv()
    score_part(1, 1)
    score_part(1, 0)
    template_copies.wait_send()
    for g in range(2):
        image_copies(g).wait_send()
        swap(g, pix).wait_send()
    blocks(NZ - 1, 0).wait_send()
    for h in range(2):
        srecv[h, pl.ds(slot(me), 1)] = ssend[h, pl.ds(slot(me), 1)]

    def logit_copy(h):
        return remote(lsend.at[h], lrecv.at[h], l_s.at[h], l_r.at[h], twin)

    chosen = (lax.broadcasted_iota(jnp.int32, (8, side), 1) < 3).astype(f32).astype(bf16)
    for h in range(2):
        norm = lax.dot_general(
            chosen,
            tall[h * half : (h + 1) * half, :, full:].reshape(ntpl, side),
            NT,
            preferred_element_type=f32,
        )
        gain = prec * lax.rsqrt(norm[:1] + 1e-06)
        score_copies(h).wait_recv()
        lsend[h] = gain * jnp.sum(srecv[h], axis=0)
        logit_copy(h).start()
    own_top = jnp.max(jnp.maximum(lsend[0], lsend[1]), axis=1, keepdims=True)
    for h in range(2):
        logit_copy(h).wait_recv()
    top = jnp.maximum(
        own_top, jnp.max(jnp.maximum(lrecv[0], lrecv[1]), axis=1, keepdims=True)
    )
    weights = [jnp.exp(lsend[h] - top) for h in range(2)]
    totals = jnp.sum(weights[0] + weights[1], axis=1, keepdims=True) + jnp.sum(
        jnp.exp(lrecv[0] - top) + jnp.exp(lrecv[1] - top), axis=1, keepdims=True
    )

    def resp_copy(h, q):
        mine = rall.at[h, slot(me)]
        return remote(mine, mine, r_s.at[h], r_r.at[h], mate(q))

    def resp_copies(h):
        some = rall.at[h, pl.ds(0, others)]
        return joint(some, some, r_s.at[h], r_r.at[h])

    for h in (1, 0):
        rall[h, pl.ds(slot(me), 1)] = (weights[h] / totals).astype(bf16)[None]
        each(lambda q: resp_copy(h, q).start())
    column = top + jnp.log(totals)
    eye = lax.broadcasted_iota(jnp.int32, (nimg, nimg), 0) == lax.broadcasted_iota(
        jnp.int32, (nimg, nimg), 1
    )
    loglik[...] = jnp.sum(jnp.where(eye, column, 0.0), axis=0, keepdims=True)

    for h in range(2):
        score_copies(h).wait_send()
        logit_copy(h).wait_send()

    near = {dst: (base, -step) for base in RELAY for dst, step in RELAY[base]}

    def near_copy(k):
        base, step = near[k]
        return remote(sums.at[POS[k]], rr.at[k], z_s, z_r.at[BASE[base]], along(step))

    def near_copies(count, base):
        return joint(sums.at[pl.ds(0, count)], rr.at[pl.ds(0, count)], z_s, z_r.at[BASE[base]])

    def far_copy(b):
        j = BASE[b]
        return remote(r2_send.at[j], r2_recv.at[j], z2_s.at[j], z2_r.at[j], along(FAR[b]))

    def base_sum(b):
        val = own_sums[BASE[b]]
        near_copies(len(RELAY[b]), b).wait_recv()
        for k, step in RELAY[b]:
            val = val + rr[k].astype(f32)
        return val

    def send_far(b):
        r2_send[BASE[b]] = base_sum(b).astype(bf16)
        far_copy(b).start()

    for h in (1, 0):
        resp_copies(h).wait_recv()
        resp = rall[h].reshape(plane * nimg, ntpl).astype(f32).T.astype(bf16)
        for c in range(2):
            res = lax.dot_general(
                resp,
                img_buf[c].reshape(plane * nimg, part),
                (((1,), (0,)), ((), ())),
                preferred_element_type=f32,
            )
            sums[h * half : (h + 1) * half, :, c * part : (c + 1) * part] = res.astype(bf16).reshape(
                half, plane, part
            )
            for k in BASE:
                i = POS[k] - h * half
                if 0 <= i < half:
                    own_sums[BASE[k], :, c * part : (c + 1) * part] = res[i * plane : (i + 1) * plane]
        for k in (ORDER[half:] if h else (13, 2, 14, 1, 15)):
            if k in near:
                near_copy(k).start()
    for h in range(2):
        resp_copies(h).wait_send()
    for b in FAR:
        send_far(b)
    val = base_sum(0)
    for b in FAR:
        far_copy(b).wait_recv()
        val = val + r2_recv[BASE[b]].astype(f32)
    for k in range(tile_rows):
        fsend[pl.ds(k, plane, stride=tile_rows), :] = val[:, k * side : (k + 1) * side]

    def final_copy(q):
        return remote(fsend.at[rows_of(q)], fin.at[rows_of(me)], f_s, f_r, mate(q))

    each(lambda q: final_copy(q).start())
    final_copies = joint(
        fsend.at[pl.ds(0, others * tile_rows)], fin.at[pl.ds(0, others * tile_rows)], f_s, f_r
    )
    fin[rows_of(me), :] = fsend[rows_of(me), :]
    near_copies(len(near), 0).wait_send()
    for b in FAR:
        far_copy(b).wait_send()
    final_copies.wait_recv()
    whole = fin[...]
    squares = jnp.sum(jnp.sum(whole * whole, axis=0, keepdims=True), axis=1, keepdims=True)
    scaled = whole * lax.rsqrt(squares / (side * side) + 1e-06)
    for q in range(plane):
        for h in range(2):
            at = q * tile_rows + h * part_rows
            stage[h, q * part_rows : (q + 1) * part_rows, :] = scaled[at : at + part_rows, :]
    half_copy = remote(stage.at[1 - pix], orecv, o_s, o_r, twin)
    half_copy.start()
    out[pl.ds(pix, 1)] = stage[pl.ds(pix, 1)]

    final_copies.wait_send()
    half_copy.wait_recv()
    out[pl.ds(1 - pix, 1)] = orecv[...][None]
    half_copy.wait_send()


def on_device(
    images,
    conformers,
    atom_types,
    type_amp,
    type_width,
    view_angles,
    template_conf,
    template_view,
    group_ids,
    group_prec,
):
    nimg, half_rows, side = images.shape
    plane = NX * NY
    part = half_rows * side // plane
    half = NZ // 2
    ntpl = half * plane
    flat = images.reshape(nimg, half_rows * side)
    bf16, f32 = jnp.bfloat16, jnp.float32
    vmem = pl.BlockSpec(memory_space=pltpu.VMEM)
    smem = pl.BlockSpec(memory_space=pltpu.SMEM)
    dma = pltpu.SemaphoreType.DMA
    natoms = atom_types.shape[0]
    averages, loglik = pl.pallas_call(
        functools.partial(em_kernel, side, min(1024, natoms)),
        out_shape=(
            jax.ShapeDtypeStruct((2, half_rows, side), f32),
            jax.ShapeDtypeStruct((1, nimg), f32),
        ),
        in_specs=[smem] * 4 + [vmem] * 6,
        out_specs=(vmem, vmem),
        scratch_shapes=[
            pltpu.VMEM((2, plane, nimg, part), bf16),
            pltpu.VMEM((2 * side, side), f32),
            pltpu.VMEM((2 * side, side), f32),
            pltpu.VMEM((NZ, plane, 2 * part + side), bf16),
            pltpu.VMEM((2, plane, nimg, ntpl), f32),
            pltpu.VMEM((2, plane, nimg, ntpl), f32),
            pltpu.VMEM((2, nimg, ntpl), f32),
            pltpu.VMEM((2, nimg, ntpl), f32),
            pltpu.VMEM((2, plane, nimg, ntpl), bf16),
            pltpu.VMEM((len(RELAY), plane, 2 * part), f32),
            pltpu.VMEM((NZ, plane, 2 * part), bf16),
            pltpu.VMEM((NZ, plane, 2 * part), bf16),
            pltpu.VMEM((len(RELAY), plane, 2 * part), bf16),
            pltpu.VMEM((len(RELAY), plane, 2 * part), bf16),
            pltpu.VMEM((side, side), f32),
            pltpu.VMEM((side, side), f32),
            pltpu.VMEM((2, half_rows, side), f32),
            pltpu.VMEM((half_rows, side), f32),
            pltpu.VMEM((side, side), f32),
            dma((2,)),
            dma((2,)),
            dma((2,)),
            dma((2,)),
            dma,
            dma,
            dma,
            dma((4,)),
            dma((2,)),
            dma((2,)),
            dma((2,)),
            dma((2,)),
            dma((2,)),
            dma((2,)),
            dma,
            dma((len(RELAY),)),
            dma((len(RELAY),)),
            dma((len(RELAY),)),
            dma,
            dma,
            dma,
            dma,
            dma,
        ],
        compiler_params=pltpu.CompilerParams(
            collective_id=0, has_side_effects=True, vmem_limit_bytes=28 * 1024 * 1024
        ),
    )(
        template_conf,
        template_view,
        type_amp,
        type_width,
        flat,
        conformers.transpose(1, 0, 2),
        atom_types[None, :],
        view_angles.T,
        group_ids[None, :],
        group_prec[None, :],
    )
    return averages, loglik[0]


def solution(mesh):
    placed = (
        P(("img", "tpl"), "pix", None),
        P(),
        P(),
        P(),
        P(),
        P(),
        P(("tpl", "img")),
        P(("tpl", "img")),
        P("img"),
        P(),
    )
    return jax.shard_map(
        on_device,
        mesh=mesh,
        in_specs=placed,
        out_specs=(P(("tpl", "img"), "pix", None), P(("img", "tpl"))),
        check_vma=False,
    )
```

```python
import functools

import jax
import jax.numpy as jnp
from jax import lax
from jax.experimental import pallas as pl
from jax.experimental.pallas import tpu as pltpu
from jax.sharding import PartitionSpec as P

NX, NY, NZL = 4, 4, 4
MESH = pl.DeviceIdType.MESH
NT = (((1,), (1,)), ((), ()))


EARLY = (0, 1, 2, 5, 11, 13, 14, 15)
LATE = (8, 3, 7, 9, 4, 6, 10, 12)
ORDER = EARLY + LATE
POS = {k: i for i, k in enumerate(ORDER)}
NZ = 16
RELAY = {
    0: ((1, -1), (15, 1), (2, -2), (14, 2)),
    5: ((8, -3), (3, 2), (7, -2), (4, 1), (6, -1)),
    11: ((13, -2), (9, 2), (10, 1), (12, -1)),
}
FAR = {5: 5, 11: -5}
BASE = {k: i for i, k in enumerate(RELAY)}
OWN_MOVES = ((0, 11, 5), (0, 5, -5), (0, 13, 3), (0, 1, -1), (0, 15, 1), (0, 2, -2), (0, 14, 2))
RELAY_MOVES = {
    5: ((5, 8, -3), (5, 3, 2), (5, 7, -2), (5, 4, 1), (5, 6, -1)),
    11: ((11, 9, 2), (11, 10, 1), (11, 12, -1)),
}
STEPS = (1, -1, 2, -2, 3, -3, 5, -5)


def em_kernel(
    side,
    kc,
    conf_sm,
    view_sm,
    tamp_sm,
    twid_sm,
    images,
    conformers,
    types,
    angles,
    ids,
    group_prec,
    out,
    loglik,
    img_buf,
    tsend,
    tbuf,
    tall,
    ssend,
    srecv,
    lsend,
    lrecv,
    rall,
    own_sums,
    sums,
    rr,
    r2_send,
    r2_recv,
    fsend,
    fin,
    stage,
    orecv,
    acc,
    i_s,
    i_r,
    x_s,
    x_r,
    t_s,
    t_r,
    a_s,
    a_r,
    s_s,
    s_r,
    l_s,
    l_r,
    r_s,
    r_r,
    z_s,
    z_r,
    z2_s,
    z2_r,
    f_s,
    f_r,
    o_s,
    o_r,
    own_sem,
):
    f32, bf16 = jnp.float32, jnp.bfloat16
    plane = NX * NY
    img = lax.axis_index("img")
    tpl = lax.axis_index("tpl")
    pix = lax.axis_index("pix")
    x = lax.rem(img, NX)
    zl = lax.rem(lax.div(img, NX), NZL)
    y = lax.div(img, NX * NZL)
    z = tpl * NZL + zl
    me = y * NX + x
    half_rows = side // 2
    part_rows = half_rows // plane
    part = part_rows * side
    tile_rows = 2 * part_rows
    nimg = images.shape[0]
    half = len(EARLY)
    ntpl = half * plane
    full = 2 * part
    tile = 2 * tile_rows

    def mate(q):
        qy = lax.div(q, NX)
        qx = lax.rem(q, NX)
        return ((qy * NZL + zl) * NX + qx, tpl, pix)

    def along(step):
        zz = lax.rem(z + step + NZ, NZ)
        zt = lax.div(zz, NZL)
        zr = lax.rem(zz, NZL)
        return ((y * NZL + zr) * NX + x, zt, pix)

    twin = (img, tpl, 1 - pix)

    def rows_of(q):
        return pl.ds(pl.multiple_of(q * tile_rows, tile_rows), tile_rows)

    def tile_of(q):
        return pl.ds(pl.multiple_of(q * tile, tile), tile)

    def slot(q):
        return lax.rem(q, 2) * (plane // 2) + lax.div(q, 2)

    def remote(src, dst, ss, rs, dev):
        return pltpu.make_async_remote_copy(
            src_ref=src, dst_ref=dst, send_sem=ss, recv_sem=rs, device_id=dev, device_id_type=MESH
        )

    def joint(src, dst, ss, rs):
        return remote(src, dst, ss, rs, twin)

    others = plane - 1

    def each(body, first=1, last=plane, step=1):
        @pl.loop(first, last, step=step, unroll=True)
        def _(d):
            body(lax.rem(me + d, plane))

    bar = pltpu.get_barrier_semaphore()
    each(lambda q: pl.semaphore_signal(bar, inc=1, device_id=mate(q), device_id_type=MESH))
    for step in STEPS:
        pl.semaphore_signal(bar, inc=1, device_id=along(step), device_id_type=MESH)
    pl.semaphore_signal(bar, inc=1, device_id=twin, device_id_type=MESH)

    def image_part(q):
        return images.at[:, pl.ds(pl.multiple_of(q * part, part), part)]

    own = pltpu.make_async_copy(image_part(me), img_buf.at[pix, slot(me)], own_sem)
    own.start()

    conf = conf_sm[pix]
    views = lax.broadcasted_iota(jnp.int32, angles.shape, 1)
    view = jnp.sum(jnp.where(views == view_sm[pix], angles[...], 0.0), axis=1, keepdims=True)
    cosines = jnp.cos(view)
    sines = jnp.sin(view)
    cos_phi, cos_theta, cos_psi = (cosines[i : i + 1, :] for i in range(3))
    sin_phi, sin_theta, sin_psi = (sines[i : i + 1, :] for i in range(3))
    r00 = cos_phi * cos_theta * cos_psi - sin_phi * sin_psi
    r01 = -cos_phi * cos_theta * sin_psi - sin_phi * cos_psi
    r02 = cos_phi * sin_theta
    r10 = sin_phi * cos_theta * cos_psi + cos_phi * sin_psi
    r11 = -sin_phi * cos_theta * sin_psi + cos_phi * cos_psi
    r12 = sin_phi * sin_theta
    s_idx = lax.broadcasted_iota(jnp.int32, (side, 1), 0)
    owner = s_idx // tile_rows
    in_tile = lax.rem(s_idx, tile_rows)
    row_id = (in_tile // part_rows) * half_rows + owner * part_rows + lax.rem(in_tile, part_rows)
    row_pos = row_id.astype(f32) - side * 0.5 + 0.5
    col_pos = s_idx.astype(f32) - side * 0.5 + 0.5
    acc[...] = jnp.zeros_like(acc)

    @pl.loop(0, types.shape[1] // kc)
    def _(k):
        sl = pl.ds(pl.multiple_of(k * kc, kc), kc)
        kind = types[:, sl]
        amp = jnp.zeros((1, kc), f32)
        width = jnp.zeros((1, kc), f32)
        for j in range(tamp_sm.shape[0]):
            amp = jnp.where(kind == j, tamp_sm[j], amp)
            width = jnp.where(kind == j, twid_sm[j], width)
        amp = amp * 0.0625
        spread = 0.5 / (width * width)
        c0, c1, c2 = (conformers[i, pl.ds(conf, 1), sl] for i in range(3))
        across = r00 * c0 + r01 * c1 + r02 * c2
        below = r10 * c0 + r11 * c1 + r12 * c2
        dc = col_pos - across
        dr = row_pos - below
        col = jnp.exp(-(dc * dc) * spread)
        row = amp * jnp.exp(-(dr * dr) * spread)
        col_hi = col.astype(bf16)
        col_lo = (col - col_hi.astype(f32)).astype(bf16)
        row_hi = row.astype(bf16)
        row_lo = (row - row_hi.astype(f32)).astype(bf16)
        total = lax.dot_general(row_hi, col_lo, NT, preferred_element_type=f32)
        total += lax.dot_general(row_lo, col_hi, NT, preferred_element_type=f32)
        total += lax.dot_general(row_hi, col_hi, NT, preferred_element_type=f32)
        acc[...] += total

    rendered = acc[...].astype(bf16).astype(f32)
    square = rendered * rendered
    norm = jnp.sum(jnp.sum(square, axis=0, keepdims=True), axis=1, keepdims=True)
    for q in range(plane):
        tsend[q * tile : q * tile + tile_rows, :] = rendered[q * tile_rows : (q + 1) * tile_rows, :]
        tsend[q * tile + tile_rows : (q + 1) * tile, :] = jnp.broadcast_to(norm, (tile_rows, side))

    groups = ids.shape[1]
    at_row = lax.broadcasted_iota(jnp.int32, (nimg, groups), 0)
    at_col = lax.broadcasted_iota(jnp.int32, (nimg, groups), 1)
    own_id = jnp.sum(
        jnp.where(at_col == at_row + tpl * nimg, ids[...].astype(f32), 0.0), axis=1, keepdims=True
    )
    ngrp = group_prec.shape[1]
    grp = lax.broadcasted_iota(jnp.int32, (nimg, ngrp), 1).astype(f32)
    prec = jnp.sum(jnp.where(grp == own_id, group_prec[...], 0.0), axis=1, keepdims=True)

    pl.semaphore_wait(bar, plane - 1 + len(STEPS) + 1)

    def template_copy(q):
        return remote(tsend.at[tile_of(q)], tbuf.at[tile_of(me)], t_s, t_r, mate(q))

    each(lambda q: template_copy(q).start())
    template_copies = joint(
        tsend.at[pl.ds(0, others * tile)], tbuf.at[pl.ds(0, others * tile)], t_s, t_r
    )

    def image_copy(q, g):
        return remote(image_part(q), img_buf.at[pix, slot(me)], i_s.at[g], i_r.at[g], mate(q))

    def image_copies(g):
        some = img_buf.at[pix, pl.ds(0, plane // 2 - 1 + g)]
        return joint(some, some, i_s.at[g], i_r.at[g])

    each(lambda q: image_copy(q, 1).start(), 1, plane, 2)

    def swap(g, h):
        some = img_buf.at[h, pl.ds(lax.rem(me + g, 2) * (plane // 2), plane // 2)]
        return remote(some, some, x_s.at[g], x_r.at[g], twin)

    tbuf[tile_of(me), :] = tsend[tile_of(me), :]
    template_copies.wait_recv()
    for k in range(tile_rows):
        tall[POS[0], :, k * side : (k + 1) * side] = tbuf[
            pl.ds(k, plane, stride=tile), :
        ].astype(bf16)
    norms = tbuf[pl.ds(tile_rows, plane, stride=tile), :]
    first = norms.astype(bf16).astype(f32)
    second = (norms - first).astype(bf16).astype(f32)
    third = norms - first - second
    lane = lax.broadcasted_iota(jnp.int32, (plane, side), 1)
    pieces = jnp.where(lane == 0, first, jnp.where(lane == 1, second, jnp.where(lane == 2, third, 0.0)))
    tall[POS[0], :, full:] = pieces.astype(bf16)

    def block(src, dst, step):
        way = 3 if dst in LATE else BASE.get(dst, 0)
        return remote(tall.at[POS[src]], tall.at[POS[dst]], a_s, a_r.at[way], along(step))

    def blocks(count, way):
        return joint(tall.at[pl.ds(0, count)], tall.at[pl.ds(0, count)], a_s, a_r.at[way])

    def relay(k):
        blocks(1, BASE[k]).wait_recv()
        for m in RELAY_MOVES[k]:
            block(*m).start()

    for m in OWN_MOVES:
        block(*m).start()
    each(lambda q: image_copy(q, 0).start(), 2, plane, 2)

    def score_copy(h, q, src_of):
        return remote(
            ssend.at[h, slot(q)], srecv.at[h, slot(src_of)], s_s.at[h], s_r.at[h], mate(q)
        )

    def score_copies(h):
        return joint(
            ssend.at[h, pl.ds(0, others)], srecv.at[h, pl.ds(0, others)], s_s.at[h], s_r.at[h]
        )

    group = 8

    def score_part(h, odd):
        base = lax.rem(me + odd, 2) * (plane // 2)

        @pl.loop(0, plane // 2 // group)
        def _(g):
            at = pl.ds(base + g * group, group)
            res = jnp.zeros((group * nimg, ntpl), f32)
            for c in range(2):
                res += lax.dot_general(
                    img_buf[c, at].reshape(group * nimg, part),
                    tall[h * half : (h + 1) * half, :, c * part : (c + 1) * part].reshape(ntpl, part),
                    NT,
                    preferred_element_type=f32,
                )
            ssend[h, at] = res.reshape(group, nimg, ntpl)

        each(lambda q: score_copy(h, q, me).start(), 2 - odd, plane, 2)

    image_copies(1).wait_recv()
    swap(1, pix).start()
    relay(5)
    relay(11)
    blocks(len(EARLY) - len(BASE), 0).wait_recv()
    swap(1, 1 - pix).wait_recv()
    score_part(0, 1)
    image_copies(0).wait_recv()
    own.wait()
    swap(0, pix).start()
    swap(0, 1 - pix).wait_recv()
    score_part(0, 0)
    blocks(len(LATE), 3).wait_recv()
    score_part(1, 1)
    score_part(1, 0)
    template_copies.wait_send()
    for g in range(2):
        image_copies(g).wait_send()
        swap(g, pix).wait_send()
    blocks(NZ - 1, 0).wait_send()
    for h in range(2):
        srecv[h, pl.ds(slot(me), 1)] = ssend[h, pl.ds(slot(me), 1)]

    def logit_copy(h):
        return remote(lsend.at[h], lrecv.at[h], l_s.at[h], l_r.at[h], twin)

    chosen = (lax.broadcasted_iota(jnp.int32, (8, side), 1) < 3).astype(f32).astype(bf16)
    for h in range(2):
        norm = lax.dot_general(
            chosen,
            tall[h * half : (h + 1) * half, :, full:].reshape(ntpl, side),
            NT,
            preferred_element_type=f32,
        )
        gain = prec * lax.rsqrt(norm[:1] + 1e-06)
        score_copies(h).wait_recv()
        lsend[h] = gain * jnp.sum(srecv[h], axis=0)
        logit_copy(h).start()
    own_top = jnp.max(jnp.maximum(lsend[0], lsend[1]), axis=1, keepdims=True)
    for h in range(2):
        logit_copy(h).wait_recv()
    top = jnp.maximum(
        own_top, jnp.max(jnp.maximum(lrecv[0], lrecv[1]), axis=1, keepdims=True)
    )
    weights = [jnp.exp(lsend[h] - top) for h in range(2)]
    totals = jnp.sum(weights[0] + weights[1], axis=1, keepdims=True) + jnp.sum(
        jnp.exp(lrecv[0] - top) + jnp.exp(lrecv[1] - top), axis=1, keepdims=True
    )

    def resp_copy(h, q):
        mine = rall.at[h, slot(me)]
        return remote(mine, mine, r_s.at[h], r_r.at[h], mate(q))

    def resp_copies(h):
        some = rall.at[h, pl.ds(0, others)]
        return joint(some, some, r_s.at[h], r_r.at[h])

    for h in (1, 0):
        rall[h, pl.ds(slot(me), 1)] = (weights[h] / totals).astype(bf16)[None]
        each(lambda q: resp_copy(h, q).start())
    column = top + jnp.log(totals)
    eye = lax.broadcasted_iota(jnp.int32, (nimg, nimg), 0) == lax.broadcasted_iota(
        jnp.int32, (nimg, nimg), 1
    )
    loglik[...] = jnp.sum(jnp.where(eye, column, 0.0), axis=0, keepdims=True)

    for h in range(2):
        score_copies(h).wait_send()
        logit_copy(h).wait_send()

    near = {dst: (base, -step) for base in RELAY for dst, step in RELAY[base]}

    def near_copy(k):
        base, step = near[k]
        return remote(sums.at[POS[k]], rr.at[k], z_s, z_r.at[BASE[base]], along(step))

    def near_copies(count, base):
        return joint(sums.at[pl.ds(0, count)], rr.at[pl.ds(0, count)], z_s, z_r.at[BASE[base]])

    def far_copy(b):
        j = BASE[b]
        return remote(r2_send.at[j], r2_recv.at[j], z2_s.at[j], z2_r.at[j], along(FAR[b]))

    def base_sum(b):
        val = own_sums[BASE[b]]
        near_copies(len(RELAY[b]), b).wait_recv()
        for k, step in RELAY[b]:
            val = val + rr[k].astype(f32)
        return val

    def send_far(b):
        r2_send[BASE[b]] = base_sum(b).astype(bf16)
        far_copy(b).start()

    for h in (1, 0):
        resp_copies(h).wait_recv()
        resp = rall[h].reshape(plane * nimg, ntpl).astype(f32).T.astype(bf16)
        for c in range(2):
            res = lax.dot_general(
                resp,
                img_buf[c].reshape(plane * nimg, part),
                (((1,), (0,)), ((), ())),
                preferred_element_type=f32,
            )
            sums[h * half : (h + 1) * half, :, c * part : (c + 1) * part] = res.astype(bf16).reshape(
                half, plane, part
            )
            for k in BASE:
                i = POS[k] - h * half
                if 0 <= i < half:
                    own_sums[BASE[k], :, c * part : (c + 1) * part] = res[i * plane : (i + 1) * plane]
        for k in (ORDER[half:] if h else (13, 2, 14, 1, 15)):
            if k in near:
                near_copy(k).start()
    for h in range(2):
        resp_copies(h).wait_send()
    for b in FAR:
        send_far(b)
    val = base_sum(0)
    for b in FAR:
        far_copy(b).wait_recv()
        val = val + r2_recv[BASE[b]].astype(f32)
    for k in range(tile_rows):
        fsend[pl.ds(k, plane, stride=tile_rows), :] = val[:, k * side : (k + 1) * side]

    def final_copy(q):
        return remote(fsend.at[rows_of(q)], fin.at[rows_of(me)], f_s, f_r, mate(q))

    each(lambda q: final_copy(q).start())
    final_copies = joint(
        fsend.at[pl.ds(0, others * tile_rows)], fin.at[pl.ds(0, others * tile_rows)], f_s, f_r
    )
    fin[rows_of(me), :] = fsend[rows_of(me), :]
    near_copies(len(near), 0).wait_send()
    for b in FAR:
        far_copy(b).wait_send()
    final_copies.wait_recv()
    whole = fin[...]
    squares = jnp.sum(jnp.sum(whole * whole, axis=0, keepdims=True), axis=1, keepdims=True)
    scaled = whole * lax.rsqrt(squares / (side * side) + 1e-06)
    for q in range(plane):
        for h in range(2):
            at = q * tile_rows + h * part_rows
            stage[h, q * part_rows : (q + 1) * part_rows, :] = scaled[at : at + part_rows, :]
    half_copy = remote(stage.at[1 - pix], orecv, o_s, o_r, twin)
    half_copy.start()
    out[pl.ds(pix, 1)] = stage[pl.ds(pix, 1)]

    final_copies.wait_send()
    half_copy.wait_recv()
    out[pl.ds(1 - pix, 1)] = orecv[...][None]
    half_copy.wait_send()


def on_device(
    images,
    conformers,
    atom_types,
    type_amp,
    type_width,
    view_angles,
    template_conf,
    template_view,
    group_ids,
    group_prec,
):
    nimg, half_rows, side = images.shape
    plane = NX * NY
    part = half_rows * side // plane
    half = NZ // 2
    ntpl = half * plane
    flat = images.reshape(nimg, half_rows * side)
    bf16, f32 = jnp.bfloat16, jnp.float32
    vmem = pl.BlockSpec(memory_space=pltpu.VMEM)
    smem = pl.BlockSpec(memory_space=pltpu.SMEM)
    dma = pltpu.SemaphoreType.DMA
    natoms = atom_types.shape[0]
    averages, loglik = pl.pallas_call(
        functools.partial(em_kernel, side, min(1024, natoms)),
        out_shape=(
            jax.ShapeDtypeStruct((2, half_rows, side), f32),
            jax.ShapeDtypeStruct((1, nimg), f32),
        ),
        in_specs=[smem] * 4 + [vmem] * 6,
        out_specs=(vmem, vmem),
        scratch_shapes=[
            pltpu.VMEM((2, plane, nimg, part), bf16),
            pltpu.VMEM((2 * side, side), f32),
            pltpu.VMEM((2 * side, side), f32),
            pltpu.VMEM((NZ, plane, 2 * part + side), bf16),
            pltpu.VMEM((2, plane, nimg, ntpl), f32),
            pltpu.VMEM((2, plane, nimg, ntpl), f32),
            pltpu.VMEM((2, nimg, ntpl), f32),
            pltpu.VMEM((2, nimg, ntpl), f32),
            pltpu.VMEM((2, plane, nimg, ntpl), bf16),
            pltpu.VMEM((len(RELAY), plane, 2 * part), f32),
            pltpu.VMEM((NZ, plane, 2 * part), bf16),
            pltpu.VMEM((NZ, plane, 2 * part), bf16),
            pltpu.VMEM((len(RELAY), plane, 2 * part), bf16),
            pltpu.VMEM((len(RELAY), plane, 2 * part), bf16),
            pltpu.VMEM((side, side), f32),
            pltpu.VMEM((side, side), f32),
            pltpu.VMEM((2, half_rows, side), f32),
            pltpu.VMEM((half_rows, side), f32),
            pltpu.VMEM((side, side), f32),
            dma((2,)),
            dma((2,)),
            dma((2,)),
            dma((2,)),
            dma,
            dma,
            dma,
            dma((4,)),
            dma((2,)),
            dma((2,)),
            dma((2,)),
            dma((2,)),
            dma((2,)),
            dma((2,)),
            dma,
            dma((len(RELAY),)),
            dma((len(RELAY),)),
            dma((len(RELAY),)),
            dma,
            dma,
            dma,
            dma,
            dma,
        ],
        compiler_params=pltpu.CompilerParams(
            collective_id=0, has_side_effects=True, vmem_limit_bytes=28 * 1024 * 1024
        ),
    )(
        template_conf,
        template_view,
        type_amp,
        type_width,
        flat,
        conformers.transpose(1, 0, 2),
        atom_types[None, :],
        view_angles.T,
        group_ids[None, :],
        group_prec[None, :],
    )
    return averages, loglik[0]


def solution(mesh):
    placed = (
        P(("img", "tpl"), "pix", None),
        P(),
        P(),
        P(),
        P(),
        P(),
        P(("tpl", "img")),
        P(("tpl", "img")),
        P("img"),
        P(),
    )
    return jax.shard_map(
        on_device,
        mesh=mesh,
        in_specs=placed,
        out_specs=(P(("tpl", "img"), "pix", None), P(("img", "tpl"))),
        check_vma=False,
    )
```
